32 devices in a mesh: view: 4 (over y, x), tile: 8 (over z, core).
Axes of the slice: x: 2, y: 2, z: 4, core: 2. Of those that a mesh axis runs over, the one named last changes fastest.
Arguments:
- estimate: float32 [256, 64, 256], P('tile'), may hold values from 0.5 to 2
- measured: bfloat16 [4, 256, 64, 256], P('view', 'tile'), may hold values from 0.5 to 2
- blur_profile: float32 [4, 256], P('view'), may hold values from 0.1 to 1
- view_offset: int32 [4], P('view'), may hold values from -6 to 6, as said below
- tile_shift: int32 [4], P('view'), may hold values from 0 to 7
Outputs:
- updated: float32 [256, 64, 256], P('tile')
The draws below stay inside these ranges and needn't reach their ends.
Inputs may be any that keep to these rules, and one draw needn't show every extreme that they name: `view_offset`: some view has offset 6 and some other view has offset -6.
All inputs are finite; a program needn't handle non-finite values.
Results may differ from the reference program's by a relative error of at most 0.0016.
Values may be sent and summed in bfloat16 or wider, within the bound.
A program may use at most 64 MiB of HBM per device.

```python
import math
import jax
import jax.numpy as jnp

CX = 32
CY = 64
CZ = 256
H = 6
VIEWS = 4
NX = 256
N_TILE = 8


def draw_view_offset(key, part):
    offsets = jax.random.randint(key, (VIEWS,), -H, H + 1)
    chosen_views = jax.random.permutation(jax.random.fold_in(key, 7), VIEWS)
    offsets = offsets.at[chosen_views[0]].set(H)
    offsets = offsets.at[chosen_views[1]].set(-H)
    return offsets.astype(jnp.int32)


def draw_measured(key, part):
    shape = (VIEWS, NX, CY, CZ)
    exponent = jax.random.uniform(key, shape, jnp.float32, math.log(0.5), math.log(2.0))
    values = jnp.exp(exponent)
    return jnp.clip(values, 0.5, 2.0).astype(jnp.bfloat16)


def with_ends(result, rng, low, top_value):
    spot = [jax.random.randint(jax.random.fold_in(rng, axis), (), 0, length) for axis, length in enumerate(result.shape)]
    main_axis = result.shape.index(max(result.shape))
    beside = spot[:main_axis] + [(spot[main_axis] + 1) % result.shape[main_axis]] + spot[main_axis + 1:]
    return result.at[tuple(spot)].set(low).at[tuple(beside)].set(top_value)


def shard_levels(rng, extent, pieces, smallest, largest):
    factor_of, own = 1.0, jax.random.fold_in(rng, 6)
    for dim, blocks in pieces:
        heights = jnp.exp(jax.random.uniform(jax.random.fold_in(own, dim), (blocks,), jnp.float32, smallest / len(pieces), largest / len(pieces)))
        factor_of = factor_of * jnp.repeat(heights, extent[dim] // blocks).reshape([-1 if axis == dim else 1 for axis in range(len(extent))])
    return factor_of


def setup_inputs(seed: int = 0) -> dict:
    keys = jax.random.split(jax.random.key(seed), 6)
    return {
        "estimate": jnp.clip(jnp.exp(math.log(2.0) - 1.3862944 * jax.random.uniform(keys[0], (NX, CY, CZ), jnp.float32) ** shard_levels(keys[0], (NX, CY, CZ), ((0, 8),), -0.2, 0.2)), 0.5, 2.0),
        "measured": draw_measured(jax.random.fold_in(keys[5], 71), 0),
        "blur_profile": jnp.clip(jnp.exp(math.log(1.0) - 2.3025851 * jax.random.uniform(keys[2], (VIEWS, CZ), jnp.float32) ** shard_levels(keys[2], (VIEWS, CZ), ((0, 4),), -0.2, 0.2)), 0.1, 1.0),
        "view_offset": draw_view_offset(jax.random.fold_in(keys[5], 71), 0),
        "tile_shift": with_ends(jax.random.randint(keys[4], (VIEWS,), 0, N_TILE), jax.random.fold_in(keys[4], 1), 0, N_TILE - 1).astype(jnp.int32),
    }


profile_sigma = 48.0


def make_kernel(profile):
    length = profile.shape[0]
    column = jnp.arange(length)
    distance = jnp.minimum(column, length - column).astype(jnp.float32)
    weights = profile * jnp.exp(-distance * distance / (2.0 * profile_sigma * profile_sigma))
    return weights / jnp.sum(weights)


def reference(estimate, measured, blur_profile, view_offset, tile_shift):
    log_total = jnp.zeros(estimate.shape, jnp.float32)
    for view_index in range(VIEWS):
        kernel = make_kernel(blur_profile[view_index])
        spectrum = jnp.fft.fft(kernel)
        blend_weight = (view_index + 1) / (VIEWS + 1)
        travel = tile_shift[view_index] * CX + view_offset[view_index]
        warped = blend_weight * jnp.roll(estimate, -travel, axis=0) + (1 - blend_weight) * jnp.roll(estimate, -travel - 1, axis=0)
        forward = jnp.real(jnp.fft.ifft(jnp.fft.fft(warped, axis=-1) * spectrum, axis=-1)).astype(jnp.float32)
        ratios = measured[view_index].astype(jnp.float32) / forward
        back = jnp.real(jnp.fft.ifft(jnp.fft.fft(ratios, axis=-1) * jnp.conj(spectrum), axis=-1)).astype(jnp.float32)
        correction = blend_weight * jnp.roll(back, travel, axis=0) + (1 - blend_weight) * jnp.roll(back, travel + 1, axis=0)
        log_total = log_total + jnp.log(correction)
    return estimate * jnp.exp(log_total)
```

```python
import functools
import math

import jax
import jax.numpy as jnp
from jax import lax
from jax.experimental import pallas as pl
from jax.experimental.pallas import tpu as pltpu
from jax.sharding import PartitionSpec as P

H = 6
TAIL, HEAD = H + 1, H
RADIX = 8
MESH = pl.DeviceIdType.MESH
ANY = pl.BlockSpec(memory_space=pl.ANY)
VMEM = pl.BlockSpec(memory_space=pltpu.VMEM)

profile_sigma = 48.0


def greet(partners):
    barrier = pltpu.get_barrier_semaphore()
    for partner in partners:
        pl.semaphore_signal(barrier, inc=1, device_id=partner, device_id_type=MESH)
    return lambda: pl.semaphore_wait(barrier, len(partners))


def exchange_kernel(views, tiles, meas, est, info, padded, edges, infos, own, send, recv, local):
    v, t = lax.axis_index("view"), lax.axis_index("tile")
    rows = meas.shape[0]
    after, before = lax.rem(t + 1, tiles), lax.rem(t + tiles - 1, tiles)
    peers = [lax.rem(v + step, views) for step in range(views)]
    partners = [(q, at) for q in peers for at in (t, after, before)][1:]
    greet(partners)()
    copies = []

    def push(src, dst, kind, step, device):
        copy = pltpu.make_async_remote_copy(
            src_ref=src, dst_ref=dst, send_sem=send.at[kind, step], recv_sem=recv.at[kind, step],
            device_id=device, device_id_type=MESH)
        copy.start()
        copies.append(copy)

    for step in range(1, views):
        push(info, infos.at[v], 3, step, (peers[step], t))
    for step in range(1, views):
        push(meas.at[:, peers[step]], padded.at[v, pl.ds(TAIL, rows)], 0, step, (peers[step], t))
    for step, q in enumerate(peers):
        push(meas.at[pl.ds(rows - TAIL, TAIL), q], padded.at[v, pl.ds(0, TAIL)], 1, step, (q, after))
        push(meas.at[pl.ds(0, HEAD), q], padded.at[v, pl.ds(TAIL + rows, HEAD)], 2, step, (q, before))
    push(est.at[pl.ds(rows - 1, 1), v], edges.at[pl.ds(0, 1)], 4, 0, (v, after))
    push(est.at[pl.ds(0, 1), v], edges.at[pl.ds(1, 1)], 4, 1, (v, before))
    kept = [
        pltpu.make_async_copy(meas.at[:, v], padded.at[v, pl.ds(TAIL, rows)], local.at[0]),
        pltpu.make_async_copy(info, infos.at[v], local.at[1]),
        pltpu.make_async_copy(est.at[:, v], own, local.at[2]),
    ]
    for copy in kept:
        copy.start()
    for copy in kept:
        copy.wait()
    for copy in copies:
        copy.wait()


def split(value):
    high = value.astype(jnp.bfloat16)
    return high, (value - high.astype(jnp.float32)).astype(jnp.bfloat16)


def blur(value, high, low, adjoint):
    dims = (((1,), (1 if adjoint else 0,)), ((), ()))
    dot = functools.partial(lax.dot_general, dimension_numbers=dims, preferred_element_type=jnp.float32)
    top, rest = split(value)
    return dot(top, high) + (dot(rest, high) + dot(top, low))


def update_kernel(views, chunk, scale, *refs):
    windows = refs[:views]
    own, edges, infos, codes = refs[views:views + 4]
    est, high, low, coded, send, recv, local = refs[views + 4:]
    v, t = lax.axis_index("view"), lax.axis_index("tile")
    rows, share, length = own.shape
    peers = [lax.rem(v + step, views) for step in range(views)]
    arrived = greet([(q, t) for q in peers[1:]])

    est[pl.ds(0, 1)] = edges[pl.ds(0, 1)]
    est[pl.ds(1, rows)] = own[...]
    est[pl.ds(rows + 1, 1)] = edges[pl.ds(1, 1)]
    column = lax.broadcasted_iota(jnp.int32, (8, length), 1)
    distance = jnp.minimum(column, length - column).astype(jnp.float32)
    bell = jnp.exp(-distance * distance / (2.0 * profile_sigma * profile_sigma))
    for k in range(views):
        weights = infos[k] * bell
        weights = (weights / jnp.sum(weights, axis=1, keepdims=True))[0:1]
        table = pltpu.roll(jnp.broadcast_to(weights, (length, length)), 0, 1, stride=1, stride_axis=0)
        top, rest = split(table)
        high[k] = top
        low[k] = rest
    arrived()

    def copy_of(i, step):
        part = pl.ds(i * chunk, chunk)
        return pltpu.make_async_remote_copy(
            src_ref=coded.at[part], dst_ref=codes.at[part, v],
            send_sem=send.at[i, step], recv_sem=recv.at[i, step],
            device_id=(peers[step], t), device_id_type=MESH)

    def kept(i):
        part = pl.ds(i * chunk, chunk)
        return pltpu.make_async_copy(coded.at[part], codes.at[part, v], local.at[i])

    def work(i, carry):
        at = i * chunk
        product = None
        for k in range(views):
            mix = (k + 1) / (views + 1)
            warped = mix * est[pl.ds(at, chunk + 1)] + (1 - mix) * est[pl.ds(at + 1, chunk + 1)]
            flat = warped.reshape((chunk + 1) * share, length)
            forward = blur(flat, high[k], low[k], False)
            seen = windows[k][pl.ds(at, chunk + 1)].astype(jnp.float32)
            ratios = seen.reshape(flat.shape) / forward
            back = blur(ratios, high[k], low[k], True).reshape(chunk + 1, share, length)
            term = mix * back[1:] + (1 - mix) * back[:-1]
            product = term if product is None else product * term
        code = jnp.round(jnp.log(product) * scale)
        coded[pl.ds(at, chunk)] = code.astype(jnp.int32).astype(jnp.int16)
        for step in range(1, views):
            copy_of(i, step).start()
        kept(i).start()
        return carry

    lax.fori_loop(0, rows // chunk, work, 0)

    def finish(i, carry):
        for step in range(1, views):
            copy_of(i, step).wait()
        kept(i).wait()
        return carry

    lax.fori_loop(0, rows // chunk, finish, 0)


def body(estimate, measured, blur_profile, view_offset, tile_shift):
    views, tiles = lax.axis_size("view"), lax.axis_size("tile")
    rows, height, length = estimate.shape
    share = height // views
    scale = 32767.0 / (views * 1.4)
    padded_rows = TAIL + rows + HEAD
    shape = jax.ShapeDtypeStruct

    meas = measured[0].reshape(rows, views, share, length)
    est = estimate.reshape(rows, views, share, length)
    row = lax.broadcasted_iota(jnp.int32, (8, length), 0)
    info = jnp.where(row == 0, blur_profile[0][None, :],
                     jnp.where(row == 1, view_offset[0].astype(jnp.float32) + 16.0,
                               tile_shift[0].astype(jnp.float32) + 1.0))
    padded, edges, infos, own = pl.pallas_call(
        functools.partial(exchange_kernel, views, tiles),
        out_shape=[
            shape((views, padded_rows, share, length), jnp.bfloat16),
            shape((2, share, length), jnp.float32),
            shape((views, 8, length), jnp.float32),
            shape((rows, share, length), jnp.float32),
        ],
        in_specs=[ANY] * 3,
        out_specs=[ANY] * 4,
        scratch_shapes=[
            pltpu.SemaphoreType.DMA((5, max(views, 2))),
            pltpu.SemaphoreType.DMA((5, max(views, 2))),
            pltpu.SemaphoreType.DMA((3,)),
        ],
        compiler_params=pltpu.CompilerParams(collective_id=0, has_side_effects=True),
    )(meas, est, info)
    return finish_update(estimate, padded, edges, infos, own, scale)


def finish_update(estimate, padded, edges, infos, own, scale):
    views, tiles = lax.axis_size("view"), lax.axis_size("tile")
    rows, height, length = estimate.shape
    share = height // views
    shape = jax.ShapeDtypeStruct
    offsets = infos[:, 1, 0].astype(jnp.int32) - 16
    shifts = infos[:, 2, 0].astype(jnp.int32) - 1

    def moved(distance, window):
        if distance == 0:
            return window
        return lax.ppermute(window, "tile", [(i, (i + distance) % tiles) for i in range(tiles)])

    windows = []
    for k in range(views):
        window = lax.dynamic_slice_in_dim(padded[k], H - offsets[k], rows + 1, 0)
        stride = 1
        while stride < tiles:
            digits = min(RADIX, -(-tiles // stride))
            routes = [functools.partial(moved, d * stride) for d in range(digits)]
            window = lax.switch(shifts[k] // stride % digits, routes, window)
            stride *= digits
        windows.append(window)

    chunk = 8
    pieces = rows // chunk
    codes = pl.pallas_call(
        functools.partial(update_kernel, views, chunk, scale),
        out_shape=shape((rows, views, share, length), jnp.int16),
        in_specs=[VMEM] * (views + 3),
        out_specs=ANY,
        scratch_shapes=[
            pltpu.VMEM((rows + 2, share, length), jnp.float32),
            pltpu.VMEM((views, length, length), jnp.bfloat16),
            pltpu.VMEM((views, length, length), jnp.bfloat16),
            pltpu.VMEM((rows, share, length), jnp.int16),
            pltpu.SemaphoreType.DMA((pieces, views)),
            pltpu.SemaphoreType.DMA((pieces, views)),
            pltpu.SemaphoreType.DMA((pieces,)),
        ],
        compiler_params=pltpu.CompilerParams(
            collective_id=1, has_side_effects=True, vmem_limit_bytes=32 * 1024 * 1024),
    )(*windows, own, edges, infos)
    total = codes.reshape(rows, height, length).astype(jnp.float32) * (1.0 / scale)
    return estimate * jnp.exp(total)


def solution(mesh):
    placed = (
        P("tile", None, None),
        P("view", "tile", None, None),
        P("view", None),
        P("view"),
        P("view"),
    )
    return jax.shard_map(
        body, mesh=mesh, in_specs=placed, out_specs=P("tile", None, None), check_vma=False
    )
```

```python
import functools
import itertools
import math

import jax
import jax.numpy as jnp
from jax import lax
from jax.experimental import pallas as pl
from jax.experimental.pallas import tpu as pltpu
from jax.sharding import PartitionSpec as P

H = 6
TAIL, HEAD = H + 1, H
RADIX = 8
MESH = pl.DeviceIdType.MESH
ANY = pl.BlockSpec(memory_space=pl.ANY)
SMEM = pl.BlockSpec(memory_space=pltpu.SMEM)
VMEM = pl.BlockSpec(memory_space=pltpu.VMEM)

profile_sigma = 48.0


def make_plan(views, tiles):
    size = 2 if tiles <= RADIX else 1
    plan = []
    for first in range(0, views, size):
        stride = 1
        while stride < tiles:
            digits = min(RADIX, -(-tiles // stride))
            plan.append((tuple(range(first, min(first + size, views))), stride, digits))
            stride *= digits
    return plan


def greet(partners):
    barrier = pltpu.get_barrier_semaphore()
    for partner in partners:
        pl.semaphore_signal(barrier, inc=1, device_id=partner, device_id_type=MESH)
    return lambda: pl.semaphore_wait(barrier, len(partners))


def exchange_kernel(views, tiles, plan, meas, est, info, frames, edges, infos, own, offsets, *rest):
    indices, (send, recv, local) = rest[:len(plan)], rest[len(plan):]
    v, t = lax.axis_index("view"), lax.axis_index("tile")
    rows = meas.shape[0]
    after, before = lax.rem(t + 1, tiles), lax.rem(t + tiles - 1, tiles)
    peers = [lax.rem(v + step, views) for step in range(views)]
    greet([(q, t) for q in peers[1:]] + [(v, after), (v, before)])()
    copies = []

    def push(src, dst, kind, step, device):
        copy = pltpu.make_async_remote_copy(
            src_ref=src, dst_ref=dst, send_sem=send.at[kind, step], recv_sem=recv.at[kind, step],
            device_id=device, device_id_type=MESH)
        copy.start()
        copies.append(copy)

    for step in range(1, views):
        push(info, infos.at[v], 1, step, (peers[step], t))
    for step in range(1, views):
        push(meas.at[:, peers[step]], frames.at[v], 0, step, (peers[step], t))
    push(est.at[pl.ds(rows - 1, 1), v], edges.at[pl.ds(0, 1)], 2, 0, (v, after))
    push(est.at[pl.ds(0, 1), v], edges.at[pl.ds(1, 1)], 2, 1, (v, before))
    kept = [
        pltpu.make_async_copy(meas.at[:, v], frames.at[v], local.at[0]),
        pltpu.make_async_copy(info, infos.at[v], local.at[1]),
        pltpu.make_async_copy(est.at[:, v], own, local.at[2]),
    ]
    for copy in kept:
        copy.start()
    for copy in kept:
        copy.wait()
    for copy in copies:
        copy.wait()
    shifts = []
    for k in range(views):
        offsets[k] = infos[k, 1, 0].astype(jnp.int32) - 16
        shifts.append(infos[k, 2, 0].astype(jnp.int32) - 1)
    for (members, stride, digits), index in zip(plan, indices):
        total = 0
        for k in members:
            total = total * digits + shifts[k] // stride % digits
        index[0] = total


def split(value):
    high = value.astype(jnp.bfloat16)
    return high, (value - high.astype(jnp.float32)).astype(jnp.bfloat16)


def blur(value, high, low, adjoint):
    dims = (((1,), (1 if adjoint else 0,)), ((), ()))
    dot = functools.partial(lax.dot_general, dimension_numbers=dims, preferred_element_type=jnp.float32)
    top, rest = split(value)
    return dot(top, high) + (dot(rest, high) + dot(top, low))


def update_kernel(views, tiles, chunk, scale, offsets, *refs):
    windows = refs[:views]
    own, edges, infos, codes = refs[views:views + 4]
    est, high, low, frame, coded, side_send, side_recv, send, recv, local = refs[views + 4:]
    v, t = lax.axis_index("view"), lax.axis_index("tile")
    rows, share, length = own.shape
    after, before = lax.rem(t + 1, tiles), lax.rem(t + tiles - 1, tiles)
    peers = [lax.rem(v + step, views) for step in range(views)]
    greet([(q, t) for q in peers[1:]] + [(v, after), (v, before)])()
    sides = []
    for k in range(views):
        for way, (start, count, to, device) in enumerate((
            (rows - TAIL, TAIL, 0, (v, after)), (0, HEAD, TAIL + rows, (v, before)))):
            sides.append(pltpu.make_async_remote_copy(
                src_ref=windows[k].at[pl.ds(start, count)], dst_ref=frame.at[k, pl.ds(to, count)],
                send_sem=side_send.at[way, k], recv_sem=side_recv.at[way, k],
                device_id=device, device_id_type=MESH))
            sides[-1].start()
    for k in range(views):
        frame[k, pl.ds(TAIL, rows)] = windows[k][...]
    est[pl.ds(0, 1)] = edges[pl.ds(0, 1)]
    est[pl.ds(1, rows)] = own[...]
    est[pl.ds(rows + 1, 1)] = edges[pl.ds(1, 1)]
    column = lax.broadcasted_iota(jnp.int32, (8, length), 1)
    distance = jnp.minimum(column, length - column).astype(jnp.float32)
    bell = jnp.exp(-distance * distance / (2.0 * profile_sigma * profile_sigma))
    for k in range(views):
        weights = infos[k] * bell
        weights = (weights / jnp.sum(weights, axis=1, keepdims=True))[0:1]
        table = pltpu.roll(jnp.broadcast_to(weights, (length, length)), 0, 1, stride=1, stride_axis=0)
        top, rest = split(table)
        high[k] = top
        low[k] = rest
    for copy in sides:
        copy.wait()

    def copy_of(i, step):
        part = pl.ds(i * chunk, chunk)
        return pltpu.make_async_remote_copy(
            src_ref=coded.at[part], dst_ref=codes.at[part, v],
            send_sem=send.at[i, step], recv_sem=recv.at[i, step],
            device_id=(peers[step], t), device_id_type=MESH)

    def kept(i):
        part = pl.ds(i * chunk, chunk)
        return pltpu.make_async_copy(coded.at[part], codes.at[part, v], local.at[i])

    def work(i, carry):
        at = i * chunk
        product = None
        for k in range(views):
            mix = (k + 1) / (views + 1)
            warped = mix * est[pl.ds(at, chunk + 1)] + (1 - mix) * est[pl.ds(at + 1, chunk + 1)]
            flat = warped.reshape((chunk + 1) * share, length)
            forward = blur(flat, high[k], low[k], False)
            seen = frame[k, pl.ds(at + H - offsets[k], chunk + 1)].astype(jnp.float32)
            ratios = seen.reshape(flat.shape) / forward
            back = blur(ratios, high[k], low[k], True).reshape(chunk + 1, share, length)
            term = mix * back[1:] + (1 - mix) * back[:-1]
            product = term if product is None else product * term
        code = jnp.round(jnp.log(product) * scale)
        coded[pl.ds(at, chunk)] = code.astype(jnp.int32).astype(jnp.int16)
        for step in range(1, views):
            copy_of(i, step).start()
        kept(i).start()
        return carry

    lax.fori_loop(0, rows // chunk, work, 0)

    def finish(i, carry):
        for step in range(1, views):
            copy_of(i, step).wait()
        kept(i).wait()
        return carry

    lax.fori_loop(0, rows // chunk, finish, 0)


def body(estimate, measured, blur_profile, view_offset, tile_shift):
    views, tiles = lax.axis_size("view"), lax.axis_size("tile")
    rows, height, length = estimate.shape
    share = height // views
    scale = 32767.0 / (views * 1.4)
    shape = jax.ShapeDtypeStruct
    plan = make_plan(views, tiles)

    meas = measured[0].reshape(rows, views, share, length)
    est = estimate.reshape(rows, views, share, length)
    row = lax.broadcasted_iota(jnp.int32, (8, length), 0)
    info = jnp.where(row == 0, blur_profile[0][None, :],
                     jnp.where(row == 1, view_offset[0].astype(jnp.float32) + 16.0,
                               tile_shift[0].astype(jnp.float32) + 1.0))
    frames, edges, infos, own, offsets, *indices = pl.pallas_call(
        functools.partial(exchange_kernel, views, tiles, plan),
        out_shape=[
            shape((views, rows, share, length), jnp.bfloat16),
            shape((2, share, length), jnp.float32),
            shape((views, 8, length), jnp.float32),
            shape((rows, share, length), jnp.float32),
            shape((views,), jnp.int32),
        ] + [shape((1,), jnp.int32)] * len(plan),
        in_specs=[ANY] * 3,
        out_specs=[ANY, ANY, VMEM, ANY] + [SMEM] * (1 + len(plan)),
        scratch_shapes=[
            pltpu.SemaphoreType.DMA((3, max(views, 2))),
            pltpu.SemaphoreType.DMA((3, max(views, 2))),
            pltpu.SemaphoreType.DMA((3,)),
        ],
        compiler_params=pltpu.CompilerParams(collective_id=0, has_side_effects=True),
    )(meas, est, info)

    def moved(distance, window):
        if distance == 0:
            return window
        return lax.ppermute(window, "tile", [(i, (i + distance) % tiles) for i in range(tiles)])

    def route(distances, *group):
        return tuple(moved(d, window) for d, window in zip(distances, group))

    windows = [frames[k] for k in range(views)]
    for (members, stride, digits), index in zip(plan, indices):
        routes = [functools.partial(route, [stride * d for d in distances])
                  for distances in itertools.product(range(digits), repeat=len(members))]
        group = lax.switch(index[0], routes, *[windows[k] for k in members])
        for k, window in zip(members, group):
            windows[k] = window

    chunk = 8
    pieces = rows // chunk
    codes = pl.pallas_call(
        functools.partial(update_kernel, views, tiles, chunk, scale),
        out_shape=shape((rows, views, share, length), jnp.int16),
        in_specs=[SMEM] + [VMEM] * (views + 3),
        out_specs=ANY,
        scratch_shapes=[
            pltpu.VMEM((rows + 2, share, length), jnp.float32),
            pltpu.VMEM((views, length, length), jnp.bfloat16),
            pltpu.VMEM((views, length, length), jnp.bfloat16),
            pltpu.VMEM((views, TAIL + rows + HEAD, share, length), jnp.bfloat16),
            pltpu.VMEM((rows, share, length), jnp.int16),
            pltpu.SemaphoreType.DMA((2, views)),
            pltpu.SemaphoreType.DMA((2, views)),
            pltpu.SemaphoreType.DMA((pieces, views)),
            pltpu.SemaphoreType.DMA((pieces, views)),
            pltpu.SemaphoreType.DMA((pieces,)),
        ],
        compiler_params=pltpu.CompilerParams(
            collective_id=1, has_side_effects=True, vmem_limit_bytes=32 * 1024 * 1024),
    )(offsets, *windows, own, edges, infos)
    total = codes.reshape(rows, height, length).astype(jnp.float32) * (1.0 / scale)
    return estimate * jnp.exp(total)


def solution(mesh):
    placed = (
        P("tile", None, None),
        P("view", "tile", None, None),
        P("view", None),
        P("view"),
        P("view"),
    )
    return jax.shard_map(
        body, mesh=mesh, in_specs=placed, out_specs=P("tile", None, None), check_vma=False
    )
```

```python
import functools
import itertools
import math

import jax
import jax.numpy as jnp
from jax import lax
from jax.experimental import pallas as pl
from jax.experimental.pallas import tpu as pltpu
from jax.sharding import PartitionSpec as P

H = 6
TAIL, HEAD = H + 1, H
RADIX = 8
MESH = pl.DeviceIdType.MESH
ANY = pl.BlockSpec(memory_space=pl.ANY)
SMEM = pl.BlockSpec(memory_space=pltpu.SMEM)
VMEM = pl.BlockSpec(memory_space=pltpu.VMEM)

profile_sigma = 48.0


def make_plan(views, tiles):
    size = 2 if tiles <= RADIX else 1
    plan = []
    for first in range(0, views, size):
        stride = 1
        while stride < tiles:
            digits = min(RADIX, -(-tiles // stride))
            plan.append((tuple(range(first, min(first + size, views))), stride, digits))
            stride *= digits
    return plan


def greet(partners):
    barrier = pltpu.get_barrier_semaphore()
    for partner in partners:
        pl.semaphore_signal(barrier, inc=1, device_id=partner, device_id_type=MESH)
    return lambda: pl.semaphore_wait(barrier, len(partners))


def exchange_kernel(views, tiles, plan, meas, est, profile, offset, shift, *refs):
    windows, (edges, infos, offsets) = refs[:views], refs[views:views + 3]
    indices, (staged, frames, info, send, recv) = refs[views + 3:-5], refs[-5:]
    v, t = lax.axis_index("view"), lax.axis_index("tile")
    rows = meas.shape[0]
    after, before = lax.rem(t + 1, tiles), lax.rem(t + tiles - 1, tiles)
    peers = [lax.rem(v + step, views) for step in range(views)]
    arrived = greet([(q, t) for q in peers[1:]] + [(v, after), (v, before)])
    copies = []

    def push(src, dst, kind, step, device):
        copy = pltpu.make_async_remote_copy(
            src_ref=src, dst_ref=dst, send_sem=send.at[kind, step], recv_sem=recv.at[kind, step],
            device_id=device, device_id_type=MESH)
        copy.start()
        copies.append(copy)

    row = lax.broadcasted_iota(jnp.int32, info.shape, 0)
    numbers = jnp.where(row == 1, offset[0].astype(jnp.float32) + 16.0, shift[0].astype(jnp.float32) + 1.0)
    info[...] = jnp.where(row == 0, jnp.broadcast_to(profile[...], info.shape), numbers)
    for step in range(1, views):
        staged[step] = meas[:, peers[step]]
    arrived()
    for step in range(1, views):
        push(info, infos.at[v], 1, step, (peers[step], t))
    for step in range(1, views):
        push(staged.at[step], frames.at[v], 0, step, (peers[step], t))
    push(est.at[rows - 1, v], edges.at[0], 2, 0, (v, after))
    push(est.at[0, v], edges.at[1], 2, 1, (v, before))
    frames[v] = meas[:, v]
    infos[v] = info[...]
    for copy in copies:
        copy.wait()
    shifts = []
    for k in range(views):
        offsets[k] = infos[k, 1, 0].astype(jnp.int32) - 16
        shifts.append(infos[k, 2, 0].astype(jnp.int32) - 1)
    for (members, stride, digits), index in zip(plan, indices):
        total = 0
        for k in members:
            total = total * digits + shifts[k] // stride % digits
        index[0] = total
    for k in range(views):
        windows[k][...] = frames[k]


def split(value):
    high = value.astype(jnp.bfloat16)
    return high, (value - high.astype(jnp.float32)).astype(jnp.bfloat16)


def blur(value, high, low, adjoint):
    dims = (((1,), (1 if adjoint else 0,)), ((), ()))
    dot = functools.partial(lax.dot_general, dimension_numbers=dims, preferred_element_type=jnp.float32)
    top, rest = split(value)
    return dot(top, high) + (dot(rest, high) + dot(top, low))


def update_kernel(views, tiles, chunk, scale, offsets, *refs):
    windows = refs[:views]
    own, edges, infos, codes = refs[views:views + 4]
    est, high, low, frame, coded, side_send, side_recv, send, recv, local = refs[views + 4:]
    v, t = lax.axis_index("view"), lax.axis_index("tile")
    rows, _, share, length = own.shape
    after, before = lax.rem(t + 1, tiles), lax.rem(t + tiles - 1, tiles)
    peers = [lax.rem(v + step, views) for step in range(views)]
    greet([(q, t) for q in peers[1:]] + [(v, after), (v, before)])()
    sides = []
    for k in range(views):
        for way, (start, count, to, device) in enumerate((
            (rows - TAIL, TAIL, 0, (v, after)), (0, HEAD, TAIL + rows, (v, before)))):
            sides.append(pltpu.make_async_remote_copy(
                src_ref=windows[k].at[pl.ds(start, count)], dst_ref=frame.at[k, pl.ds(to, count)],
                send_sem=side_send.at[way, k], recv_sem=side_recv.at[way, k],
                device_id=device, device_id_type=MESH))
            sides[-1].start()
    for k in range(views):
        frame[k, pl.ds(TAIL, rows)] = windows[k][...]
    est[pl.ds(0, 1)] = edges[pl.ds(0, 1)]
    est[pl.ds(1, rows)] = own[:, v]
    est[pl.ds(rows + 1, 1)] = edges[pl.ds(1, 1)]
    column = lax.broadcasted_iota(jnp.int32, (8, length), 1)
    distance = jnp.minimum(column, length - column).astype(jnp.float32)
    bell = jnp.exp(-distance * distance / (2.0 * profile_sigma * profile_sigma))
    for k in range(views):
        weights = infos[k] * bell
        weights = (weights / jnp.sum(weights, axis=1, keepdims=True))[0:1]
        table = pltpu.roll(jnp.broadcast_to(weights, (length, length)), 0, 1, stride=1, stride_axis=0)
        top, rest = split(table)
        high[k] = top
        low[k] = rest

    def copy_of(i, step):
        part = pl.ds(i * chunk, chunk)
        return pltpu.make_async_remote_copy(
            src_ref=coded.at[part], dst_ref=codes.at[part, v],
            send_sem=send.at[i, step], recv_sem=recv.at[i, step],
            device_id=(peers[step], t), device_id_type=MESH)

    def kept(i):
        part = pl.ds(i * chunk, chunk)
        return pltpu.make_async_copy(coded.at[part], codes.at[part, v], local.at[i])

    def work(inner, i, carry):
        at = i * chunk
        product = None
        for k in range(views):
            mix = (k + 1) / (views + 1)
            warped = mix * est[pl.ds(at, chunk + 1)] + (1 - mix) * est[pl.ds(at + 1, chunk + 1)]
            flat = warped.reshape((chunk + 1) * share, length)
            forward = blur(flat, high[k], low[k], False)
            if inner:
                seen = windows[k][pl.ds(at - 1 - offsets[k], chunk + 1)].astype(jnp.float32)
            else:
                seen = frame[k, pl.ds(at + H - offsets[k], chunk + 1)].astype(jnp.float32)
            ratios = seen.reshape(flat.shape) / forward
            back = blur(ratios, high[k], low[k], True).reshape(chunk + 1, share, length)
            term = mix * back[1:] + (1 - mix) * back[:-1]
            product = term if product is None else product * term
        code = jnp.round(jnp.log(product) * scale)
        coded[pl.ds(at, chunk)] = code.astype(jnp.int32).astype(jnp.int16)
        for step in range(1, views):
            copy_of(i, step).start()
        kept(i).start()
        return carry

    first = -(-TAIL // chunk)
    last = max(first, (rows - HEAD) // chunk)
    lax.fori_loop(first, last, functools.partial(work, True), 0)
    for copy in sides:
        copy.wait()
    lax.fori_loop(0, first, functools.partial(work, False), 0)
    lax.fori_loop(last, rows // chunk, functools.partial(work, False), 0)

    def finish(i, carry):
        for step in range(1, views):
            copy_of(i, step).wait()
        kept(i).wait()
        return carry

    lax.fori_loop(0, rows // chunk, finish, 0)


def body(estimate, measured, blur_profile, view_offset, tile_shift):
    views, tiles = lax.axis_size("view"), lax.axis_size("tile")
    rows, height, length = estimate.shape
    share = height // views
    scale = 32767.0 / (views * 1.4)
    shape = jax.ShapeDtypeStruct
    plan = make_plan(views, tiles)

    meas = measured[0].reshape(rows, views, share, length)
    est = estimate.reshape(rows, views, share, length)
    out = pl.pallas_call(
        functools.partial(exchange_kernel, views, tiles, plan),
        out_shape=[shape((rows, share, length), jnp.bfloat16)] * views + [
            shape((2, share, length), jnp.float32),
            shape((views, 8, length), jnp.float32),
            shape((views,), jnp.int32),
        ] + [shape((1,), jnp.int32)] * len(plan),
        in_specs=[VMEM, ANY, VMEM, SMEM, SMEM],
        out_specs=[VMEM] * (views + 2) + [SMEM] * (1 + len(plan)),
        scratch_shapes=[
            pltpu.VMEM((views, rows, share, length), jnp.bfloat16),
            pltpu.VMEM((views, rows, share, length), jnp.bfloat16),
            pltpu.VMEM((8, length), jnp.float32),
            pltpu.SemaphoreType.DMA((3, max(views, 2))),
            pltpu.SemaphoreType.DMA((3, max(views, 2))),
        ],
        compiler_params=pltpu.CompilerParams(
            collective_id=0, has_side_effects=True, vmem_limit_bytes=24 * 1024 * 1024),
    )(meas, est, blur_profile, view_offset, tile_shift)
    windows, (edges, infos, offsets, *indices) = out[:views], out[views:]

    def moved(distance, window):
        if distance == 0:
            return window
        return lax.ppermute(window, "tile", [(i, (i + distance) % tiles) for i in range(tiles)])

    def route(distances, *group):
        return tuple(moved(d, window) for d, window in zip(distances, group))

    windows = list(windows)
    for (members, stride, digits), index in zip(plan, indices):
        routes = [functools.partial(route, [stride * d for d in distances])
                  for distances in itertools.product(range(digits), repeat=len(members))]
        group = lax.switch(index[0], routes, *[windows[k] for k in members])
        for k, window in zip(members, group):
            windows[k] = window

    chunk = 8
    pieces = rows // chunk
    codes = pl.pallas_call(
        functools.partial(update_kernel, views, tiles, chunk, scale),
        out_shape=shape((rows, views, share, length), jnp.int16),
        in_specs=[SMEM] + [VMEM] * (views + 3),
        out_specs=ANY,
        scratch_shapes=[
            pltpu.VMEM((rows + 2, share, length), jnp.float32),
            pltpu.VMEM((views, length, length), jnp.bfloat16),
            pltpu.VMEM((views, length, length), jnp.bfloat16),
            pltpu.VMEM((views, TAIL + rows + HEAD, share, length), jnp.bfloat16),
            pltpu.VMEM((rows, share, length), jnp.int16),
            pltpu.SemaphoreType.DMA((2, views)),
            pltpu.SemaphoreType.DMA((2, views)),
            pltpu.SemaphoreType.DMA((pieces, views)),
            pltpu.SemaphoreType.DMA((pieces, views)),
            pltpu.SemaphoreType.DMA((pieces,)),
        ],
        compiler_params=pltpu.CompilerParams(
            collective_id=1, has_side_effects=True, vmem_limit_bytes=32 * 1024 * 1024),
    )(offsets, *windows, est, edges, infos)
    updated = est * jnp.exp(codes.astype(jnp.float32) * (1.0 / scale))
    return updated.reshape(estimate.shape)


def solution(mesh):
    placed = (
        P("tile", None, None),
        P("view", "tile", None, None),
        P("view", None),
        P("view"),
        P("view"),
    )
    return jax.shard_map(
        body, mesh=mesh, in_specs=placed, out_specs=P("tile", None, None), check_vma=False
    )
```

```python
import functools
import itertools
import math

import jax
import jax.numpy as jnp
from jax import lax
from jax.experimental import pallas as pl
from jax.experimental.pallas import tpu as pltpu
from jax.sharding import PartitionSpec as P

H = 6
TAIL, HEAD = H + 1, H
RADIX = 8
MESH = pl.DeviceIdType.MESH
HBM = pl.BlockSpec(memory_space=pltpu.HBM)
ANY = pl.BlockSpec(memory_space=pl.ANY)
SMEM = pl.BlockSpec(memory_space=pltpu.SMEM)
VMEM = pl.BlockSpec(memory_space=pltpu.VMEM)

profile_sigma = 48.0


def make_plan(views, tiles):
    size = 2 if tiles <= RADIX else 1
    plan = []
    for first in range(0, views, size):
        stride = 1
        while stride < tiles:
            digits = min(RADIX, -(-tiles // stride))
            plan.append((tuple(range(first, min(first + size, views))), stride, digits))
            stride *= digits
    return plan


def greet(partners):
    barrier = pltpu.get_barrier_semaphore()
    for partner in partners:
        pl.semaphore_signal(barrier, inc=1, device_id=partner, device_id_type=MESH)
    return lambda: pl.semaphore_wait(barrier, len(partners))


def exchange_kernel(views, tiles, plan, meas, est, profile, offset, shift, *refs):
    windows, (edges, infos) = refs[:views], refs[views:views + 2]
    indices = refs[views + 2:-10]
    slab, low, high, staged, frames, weights, info, send, recv, local = refs[-10:]
    v, t = lax.axis_index("view"), lax.axis_index("tile")
    rows = meas.shape[0]
    middle = rows - 2 * H
    sides = TAIL + HEAD
    reach = low.shape[0] - TAIL
    after, before = lax.rem(t + 1, tiles), lax.rem(t + tiles - 1, tiles)
    peers = [lax.rem(v + step, views) for step in range(views)]
    arrived = greet([(q, t) for q in peers[1:]] + [(v, after), (v, before)])
    loads = [pltpu.make_async_copy(meas, slab, local.at[0]),
             pltpu.make_async_copy(profile, weights, local.at[1])]
    for copy in loads:
        copy.start()

    def push(src, dst, kind, step, device):
        copy = pltpu.make_async_remote_copy(
            src_ref=src, dst_ref=dst, send_sem=send.at[kind, step], recv_sem=recv.at[kind, step],
            device_id=device, device_id_type=MESH)
        copy.start()
        return copy

    for copy in loads:
        copy.wait()
    row = lax.broadcasted_iota(jnp.int32, info.shape, 0)
    numbers = jnp.where(row == 1, offset[0].astype(jnp.float32) + 16.0, shift[0].astype(jnp.float32) + 1.0)
    info[...] = jnp.where(row == 0, jnp.broadcast_to(weights[...], info.shape), numbers)
    move = offset[0]
    arrived()
    halos = [
        push(slab.at[pl.ds(rows - TAIL, TAIL)], low.at[pl.ds(0, TAIL)], 2, 0, (v, after)),
        push(slab.at[pl.ds(0, HEAD)], high.at[pl.ds(reach, HEAD)], 2, 1, (v, before)),
    ]
    copies = [push(info, infos.at[v], 1, step, (peers[step], t)) for step in range(1, views)]
    for step in range(1, views):
        staged[step, pl.ds(0, middle)] = slab[pl.ds(H - move, middle), peers[step]]
        copies.append(push(staged.at[step, pl.ds(0, middle)], frames.at[v, pl.ds(0, middle)], 0, step, (peers[step], t)))
    copies.append(push(est.at[rows - 1, v], edges.at[0], 4, 0, (v, after)))
    copies.append(push(est.at[0, v], edges.at[1], 4, 1, (v, before)))
    frames[v, pl.ds(0, middle)] = slab[pl.ds(H - move, middle), v]
    infos[v] = info[...]
    low[pl.ds(TAIL, reach)] = slab[pl.ds(0, reach)]
    high[pl.ds(0, reach)] = slab[pl.ds(rows - reach, reach)]
    for copy in halos:
        copy.wait()
    for step in range(1, views):
        staged[step, pl.ds(middle, TAIL)] = low[pl.ds(H - move, TAIL), peers[step]]
        staged[step, pl.ds(middle + TAIL, HEAD)] = high[pl.ds(H - move, HEAD), peers[step]]
        copies.append(push(staged.at[step, pl.ds(middle, sides)], frames.at[v, pl.ds(middle, sides)], 3, step, (peers[step], t)))
    frames[v, pl.ds(middle, TAIL)] = low[pl.ds(H - move, TAIL), v]
    frames[v, pl.ds(middle + TAIL, HEAD)] = high[pl.ds(H - move, HEAD), v]
    for copy in copies:
        copy.wait()
    shifts = [infos[k, 2, 0].astype(jnp.int32) - 1 for k in range(views)]
    for (members, stride, digits), index in zip(plan, indices):
        total = 0
        for k in members:
            total = total * digits + shifts[k] // stride % digits
        index[0] = total
    for k in range(views):
        windows[k][pl.ds(0, TAIL)] = frames[k, pl.ds(middle, TAIL)]
        windows[k][pl.ds(TAIL, middle)] = frames[k, pl.ds(0, middle)]
        windows[k][pl.ds(TAIL + middle, HEAD)] = frames[k, pl.ds(middle + TAIL, HEAD)]


def split(value):
    high = value.astype(jnp.bfloat16)
    return high, (value - high.astype(jnp.float32)).astype(jnp.bfloat16)


def blur(value, high, low, adjoint):
    dims = (((1,), (1 if adjoint else 0,)), ((), ()))
    dot = functools.partial(lax.dot_general, dimension_numbers=dims, preferred_element_type=jnp.float32)
    top, rest = split(value)
    return dot(top, high) + (dot(rest, high) + dot(top, low))


def update_kernel(views, chunk, scale, *refs):
    windows = refs[:views]
    own, edges, infos, codes = refs[views:views + 4]
    est, high, low, coded, send, recv, local = refs[views + 4:]
    v, t = lax.axis_index("view"), lax.axis_index("tile")
    rows, _, share, length = own.shape
    peers = [lax.rem(v + step, views) for step in range(views)]
    arrived = greet([(q, t) for q in peers[1:]])
    est[pl.ds(0, 1)] = edges[pl.ds(0, 1)]
    est[pl.ds(1, rows)] = own[:, v]
    est[pl.ds(rows + 1, 1)] = edges[pl.ds(1, 1)]
    column = lax.broadcasted_iota(jnp.int32, (8, length), 1)
    distance = jnp.minimum(column, length - column).astype(jnp.float32)
    bell = jnp.exp(-distance * distance / (2.0 * profile_sigma * profile_sigma))
    for k in range(views):
        weights = infos[k] * bell
        weights = (weights / jnp.sum(weights, axis=1, keepdims=True))[0:1]
        table = pltpu.roll(jnp.broadcast_to(weights, (length, length)), 0, 1, stride=1, stride_axis=0)
        top, rest = split(table)
        high[k] = top
        low[k] = rest
    arrived()

    def copy_of(i, step):
        part = pl.ds(i * chunk, chunk)
        return pltpu.make_async_remote_copy(
            src_ref=coded.at[part], dst_ref=codes.at[part, v],
            send_sem=send.at[i, step], recv_sem=recv.at[i, step],
            device_id=(peers[step], t), device_id_type=MESH)

    def kept(i):
        part = pl.ds(i * chunk, chunk)
        return pltpu.make_async_copy(coded.at[part], codes.at[part, v], local.at[i])

    def work(i, carry):
        at = i * chunk
        product = None
        for k in range(views):
            mix = (k + 1) / (views + 1)
            warped = mix * est[pl.ds(at, chunk + 1)] + (1 - mix) * est[pl.ds(at + 1, chunk + 1)]
            flat = warped.reshape((chunk + 1) * share, length)
            forward = blur(flat, high[k], low[k], False)
            seen = windows[k][pl.ds(at, chunk + 1)].astype(jnp.float32)
            ratios = seen.reshape(flat.shape) / forward
            back = blur(ratios, high[k], low[k], True).reshape(chunk + 1, share, length)
            term = mix * back[1:] + (1 - mix) * back[:-1]
            product = term if product is None else product * term
        code = jnp.round(jnp.log(product) * scale)
        coded[pl.ds(at, chunk)] = code.astype(jnp.int32).astype(jnp.int16)
        for step in range(1, views):
            copy_of(i, step).start()
        kept(i).start()
        return carry

    lax.fori_loop(0, rows // chunk, work, 0)

    def finish(i, carry):
        for step in range(1, views):
            copy_of(i, step).wait()
        kept(i).wait()
        return carry

    lax.fori_loop(0, rows // chunk, finish, 0)


def body(estimate, measured, blur_profile, view_offset, tile_shift):
    views, tiles = lax.axis_size("view"), lax.axis_size("tile")
    rows, height, length = estimate.shape
    share = height // views
    scale = 32767.0 / (views * 1.4)
    shape = jax.ShapeDtypeStruct
    plan = make_plan(views, tiles)

    meas = measured[0].reshape(rows, views, share, length)
    est = estimate.reshape(rows, views, share, length)
    out = pl.pallas_call(
        functools.partial(exchange_kernel, views, tiles, plan),
        out_shape=[shape((rows + 1, share, length), jnp.bfloat16)] * views + [
            shape((2, share, length), jnp.float32),
            shape((views, 8, length), jnp.float32),
        ] + [shape((1,), jnp.int32)] * len(plan),
        in_specs=[HBM, HBM, HBM, SMEM, SMEM],
        out_specs=[VMEM] * (views + 2) + [SMEM] * len(plan),
        scratch_shapes=[
            pltpu.VMEM((rows, views, share, length), jnp.bfloat16),
            pltpu.VMEM((TAIL + 2 * H, views, share, length), jnp.bfloat16),
            pltpu.VMEM((HEAD + 2 * H, views, share, length), jnp.bfloat16),
            pltpu.VMEM((views, rows + 1, share, length), jnp.bfloat16),
            pltpu.VMEM((views, rows + 1, share, length), jnp.bfloat16),
            pltpu.VMEM((1, length), jnp.float32),
            pltpu.VMEM((8, length), jnp.float32),
            pltpu.SemaphoreType.DMA((5, max(views, 2))),
            pltpu.SemaphoreType.DMA((5, max(views, 2))),
            pltpu.SemaphoreType.DMA((2,)),
        ],
        compiler_params=pltpu.CompilerParams(
            collective_id=0, has_side_effects=True, vmem_limit_bytes=24 * 1024 * 1024),
    )(meas, est, blur_profile, view_offset, tile_shift)
    windows, (edges, infos, *indices) = out[:views], out[views:]

    def moved(distance, window):
        if distance == 0:
            return window
        return lax.ppermute(window, "tile", [(i, (i + distance) % tiles) for i in range(tiles)])

    def route(distances, *group):
        return tuple(moved(d, window) for d, window in zip(distances, group))

    windows = list(windows)
    for (members, stride, digits), index in zip(plan, indices):
        routes = [functools.partial(route, [stride * d for d in distances])
                  for distances in itertools.product(range(digits), repeat=len(members))]
        group = lax.switch(index[0], routes, *[windows[k] for k in members])
        for k, window in zip(members, group):
            windows[k] = window

    chunk = 8
    pieces = rows // chunk
    codes = pl.pallas_call(
        functools.partial(update_kernel, views, chunk, scale),
        out_shape=shape((rows, views, share, length), jnp.int16),
        in_specs=[VMEM] * (views + 3),
        out_specs=ANY,
        scratch_shapes=[
            pltpu.VMEM((rows + 2, share, length), jnp.float32),
            pltpu.VMEM((views, length, length), jnp.bfloat16),
            pltpu.VMEM((views, length, length), jnp.bfloat16),
            pltpu.VMEM((rows, share, length), jnp.int16),
            pltpu.SemaphoreType.DMA((pieces, views)),
            pltpu.SemaphoreType.DMA((pieces, views)),
            pltpu.SemaphoreType.DMA((pieces,)),
        ],
        compiler_params=pltpu.CompilerParams(
            collective_id=1, has_side_effects=True, vmem_limit_bytes=32 * 1024 * 1024),
    )(*windows, est, edges, infos)
    updated = est * jnp.exp(codes.astype(jnp.float32) * (1.0 / scale))
    return updated.reshape(estimate.shape)


def solution(mesh):
    placed = (
        P("tile", None, None),
        P("view", "tile", None, None),
        P("view", None),
        P("view"),
        P("view"),
    )
    return jax.shard_map(
        body, mesh=mesh, in_specs=placed, out_specs=P("tile", None, None), check_vma=False
    )
```

```python
import functools
import itertools
import math

import jax
import jax.numpy as jnp
from jax import lax
from jax.experimental import pallas as pl
from jax.experimental.pallas import tpu as pltpu
from jax.sharding import PartitionSpec as P

H = 6
TAIL, HEAD = H + 1, H
RADIX = 8
MESH = pl.DeviceIdType.MESH
HBM = pl.BlockSpec(memory_space=pltpu.HBM)
ANY = pl.BlockSpec(memory_space=pl.ANY)
SMEM = pl.BlockSpec(memory_space=pltpu.SMEM)
VMEM = pl.BlockSpec(memory_space=pltpu.VMEM)

profile_sigma = 48.0


def make_plan(views, tiles):
    size = 2 if tiles <= RADIX else 1
    plan = []
    for first in range(0, views, size):
        stride = 1
        while stride < tiles:
            digits = min(RADIX, -(-tiles // stride))
            plan.append((tuple(range(first, min(first + size, views))), stride, digits))
            stride *= digits
    return plan


def greet(partners):
    barrier = pltpu.get_barrier_semaphore()
    for partner in partners:
        pl.semaphore_signal(barrier, inc=1, device_id=partner, device_id_type=MESH)
    return lambda: pl.semaphore_wait(barrier, len(partners))


def exchange_kernel(views, tiles, plan, meas, est, profile, offset, shift, *refs):
    windows, (edges, tops, rests) = refs[:views], refs[views:views + 3]
    indices, infos = refs[views + 3:-11], refs[-11]
    slab, low, high, staged, frames, weights, info, send, recv, local = refs[-10:]
    v, t = lax.axis_index("view"), lax.axis_index("tile")
    rows = meas.shape[0]
    middle = rows - 2 * H
    sides = TAIL + HEAD
    reach = low.shape[0] - TAIL
    after, before = lax.rem(t + 1, tiles), lax.rem(t + tiles - 1, tiles)
    peers = [lax.rem(v + step, views) for step in range(views)]
    arrived = greet([(q, t) for q in peers[1:]] + [(v, after), (v, before)])
    loads = [pltpu.make_async_copy(meas, slab, local.at[0]),
             pltpu.make_async_copy(profile, weights, local.at[1])]
    for copy in loads:
        copy.start()

    def push(src, dst, kind, step, device):
        copy = pltpu.make_async_remote_copy(
            src_ref=src, dst_ref=dst, send_sem=send.at[kind, step], recv_sem=recv.at[kind, step],
            device_id=device, device_id_type=MESH)
        copy.start()
        return copy

    for copy in loads:
        copy.wait()
    row = lax.broadcasted_iota(jnp.int32, info.shape, 0)
    numbers = jnp.where(row == 1, offset[0].astype(jnp.float32) + 16.0, shift[0].astype(jnp.float32) + 1.0)
    info[...] = jnp.where(row == 0, jnp.broadcast_to(weights[...], info.shape), numbers)
    move = offset[0]
    arrived()
    halos = [
        push(slab.at[pl.ds(rows - TAIL, TAIL)], low.at[pl.ds(0, TAIL)], 2, 0, (v, after)),
        push(slab.at[pl.ds(0, HEAD)], high.at[pl.ds(reach, HEAD)], 2, 1, (v, before)),
    ]
    notes = [push(info, infos.at[v], 1, step, (peers[step], t)) for step in range(1, views)]
    copies = []
    for step in range(1, views):
        staged[step, pl.ds(0, middle)] = slab[pl.ds(H - move, middle), peers[step]]
        copies.append(push(staged.at[step, pl.ds(0, middle)], frames.at[v, pl.ds(0, middle)], 0, step, (peers[step], t)))
    copies.append(push(est.at[rows - 1, v], edges.at[0], 4, 0, (v, after)))
    copies.append(push(est.at[0, v], edges.at[1], 4, 1, (v, before)))
    frames[v, pl.ds(0, middle)] = slab[pl.ds(H - move, middle), v]
    infos[v] = info[...]
    low[pl.ds(TAIL, reach)] = slab[pl.ds(0, reach)]
    high[pl.ds(0, reach)] = slab[pl.ds(rows - reach, reach)]
    for copy in halos:
        copy.wait()
    for step in range(1, views):
        staged[step, pl.ds(middle, TAIL)] = low[pl.ds(H - move, TAIL), peers[step]]
        staged[step, pl.ds(middle + TAIL, HEAD)] = high[pl.ds(H - move, HEAD), peers[step]]
        copies.append(push(staged.at[step, pl.ds(middle, sides)], frames.at[v, pl.ds(middle, sides)], 3, step, (peers[step], t)))
    frames[v, pl.ds(middle, TAIL)] = low[pl.ds(H - move, TAIL), v]
    frames[v, pl.ds(middle + TAIL, HEAD)] = high[pl.ds(H - move, HEAD), v]
    for copy in notes:
        copy.wait()
    length = meas.shape[3]
    column = lax.broadcasted_iota(jnp.int32, info.shape, 1)
    distance = jnp.minimum(column, length - column).astype(jnp.float32)
    bell = jnp.exp(-distance * distance / (2.0 * profile_sigma * profile_sigma))
    for k in range(views):
        taps = infos[k] * bell
        taps = (taps / jnp.sum(taps, axis=1, keepdims=True))[0:1]
        table = pltpu.roll(jnp.broadcast_to(taps, (length, length)), 0, 1, stride=1, stride_axis=0)
        top, rest = split(table)
        tops[k] = top
        rests[k] = rest
    shifts = [infos[k, 2, 0].astype(jnp.int32) - 1 for k in range(views)]
    for (members, stride, digits), index in zip(plan, indices):
        total = 0
        for k in members:
            total = total * digits + shifts[k] // stride % digits
        index[0] = total
    for copy in copies:
        copy.wait()
    for k in range(views):
        windows[k][pl.ds(0, TAIL)] = frames[k, pl.ds(middle, TAIL)]
        windows[k][pl.ds(TAIL, middle)] = frames[k, pl.ds(0, middle)]
        windows[k][pl.ds(TAIL + middle, HEAD)] = frames[k, pl.ds(middle + TAIL, HEAD)]


def split(value):
    high = value.astype(jnp.bfloat16)
    return high, (value - high.astype(jnp.float32)).astype(jnp.bfloat16)


def blur(value, high, low, adjoint):
    dims = (((1,), (1 if adjoint else 0,)), ((), ()))
    dot = functools.partial(lax.dot_general, dimension_numbers=dims, preferred_element_type=jnp.float32)
    top, rest = split(value)
    return dot(top, high) + (dot(rest, high) + dot(top, low))


def update_kernel(views, chunk, scale, *refs):
    windows = refs[:views]
    own, edges, high, low, codes = refs[views:views + 5]
    est, coded, send, recv, local = refs[views + 5:]
    v, t = lax.axis_index("view"), lax.axis_index("tile")
    rows, _, share, length = own.shape
    peers = [lax.rem(v + step, views) for step in range(views)]
    arrived = greet([(q, t) for q in peers[1:]])
    est[pl.ds(0, 1)] = edges[pl.ds(0, 1)]
    est[pl.ds(1, rows)] = own[:, v]
    est[pl.ds(rows + 1, 1)] = edges[pl.ds(1, 1)]
    arrived()

    def copy_of(i, step):
        part = pl.ds(i * chunk, chunk)
        return pltpu.make_async_remote_copy(
            src_ref=coded.at[part], dst_ref=codes.at[part, v],
            send_sem=send.at[i, step], recv_sem=recv.at[i, step],
            device_id=(peers[step], t), device_id_type=MESH)

    def kept(i):
        part = pl.ds(i * chunk, chunk)
        return pltpu.make_async_copy(coded.at[part], codes.at[part, v], local.at[i])

    def work(i, carry):
        at = i * chunk
        product = None
        for k in range(views):
            mix = (k + 1) / (views + 1)
            warped = mix * est[pl.ds(at, chunk + 1)] + (1 - mix) * est[pl.ds(at + 1, chunk + 1)]
            flat = warped.reshape((chunk + 1) * share, length)
            forward = blur(flat, high[k], low[k], False)
            seen = windows[k][pl.ds(at, chunk + 1)].astype(jnp.float32)
            ratios = seen.reshape(flat.shape) / forward
            back = blur(ratios, high[k], low[k], True).reshape(chunk + 1, share, length)
            term = mix * back[1:] + (1 - mix) * back[:-1]
            product = term if product is None else product * term
        code = jnp.round(jnp.log(product) * scale)
        coded[pl.ds(at, chunk)] = code.astype(jnp.int32).astype(jnp.int16)
        for step in range(1, views):
            copy_of(i, step).start()
        kept(i).start()
        return carry

    lax.fori_loop(0, rows // chunk, work, 0)

    def finish(i, carry):
        for step in range(1, views):
            copy_of(i, step).wait()
        kept(i).wait()
        return carry

    lax.fori_loop(0, rows // chunk, finish, 0)


def body(estimate, measured, blur_profile, view_offset, tile_shift):
    views, tiles = lax.axis_size("view"), lax.axis_size("tile")
    rows, height, length = estimate.shape
    share = height // views
    scale = 32767.0 / (views * 1.4)
    shape = jax.ShapeDtypeStruct
    plan = make_plan(views, tiles)

    meas = measured[0].reshape(rows, views, share, length)
    est = estimate.reshape(rows, views, share, length)
    out = pl.pallas_call(
        functools.partial(exchange_kernel, views, tiles, plan),
        out_shape=[shape((rows + 1, share, length), jnp.bfloat16)] * views + [
            shape((2, share, length), jnp.float32),
            shape((views, length, length), jnp.bfloat16),
            shape((views, length, length), jnp.bfloat16),
        ] + [shape((1,), jnp.int32)] * len(plan),
        in_specs=[HBM, HBM, HBM, SMEM, SMEM],
        out_specs=[VMEM] * (views + 3) + [SMEM] * len(plan),
        scratch_shapes=[
            pltpu.VMEM((views, 8, length), jnp.float32),
            pltpu.VMEM((rows, views, share, length), jnp.bfloat16),
            pltpu.VMEM((TAIL + 2 * H, views, share, length), jnp.bfloat16),
            pltpu.VMEM((HEAD + 2 * H, views, share, length), jnp.bfloat16),
            pltpu.VMEM((views, rows + 1, share, length), jnp.bfloat16),
            pltpu.VMEM((views, rows + 1, share, length), jnp.bfloat16),
            pltpu.VMEM((1, length), jnp.float32),
            pltpu.VMEM((8, length), jnp.float32),
            pltpu.SemaphoreType.DMA((5, max(views, 2))),
            pltpu.SemaphoreType.DMA((5, max(views, 2))),
            pltpu.SemaphoreType.DMA((2,)),
        ],
        compiler_params=pltpu.CompilerParams(
            collective_id=0, has_side_effects=True, vmem_limit_bytes=60 * 1024 * 1024),
    )(meas, est, blur_profile, view_offset, tile_shift)
    windows, (edges, tops, rests, *indices) = out[:views], out[views:]

    def moved(distance, window):
        if distance == 0:
            return window
        return lax.ppermute(window, "tile", [(i, (i + distance) % tiles) for i in range(tiles)])

    def route(distances, *group):
        return tuple(moved(d, window) for d, window in zip(distances, group))

    windows = list(windows)
    for (members, stride, digits), index in zip(plan, indices):
        routes = [functools.partial(route, [stride * d for d in distances])
                  for distances in itertools.product(range(digits), repeat=len(members))]
        group = lax.switch(index[0], routes, *[windows[k] for k in members])
        for k, window in zip(members, group):
            windows[k] = window

    chunk = 8
    pieces = rows // chunk
    codes = pl.pallas_call(
        functools.partial(update_kernel, views, chunk, scale),
        out_shape=shape((rows, views, share, length), jnp.int16),
        in_specs=[VMEM] * (views + 4),
        out_specs=ANY,
        scratch_shapes=[
            pltpu.VMEM((rows + 2, share, length), jnp.float32),
            pltpu.VMEM((rows, share, length), jnp.int16),
            pltpu.SemaphoreType.DMA((pieces, views)),
            pltpu.SemaphoreType.DMA((pieces, views)),
            pltpu.SemaphoreType.DMA((pieces,)),
        ],
        compiler_params=pltpu.CompilerParams(
            collective_id=1, has_side_effects=True, vmem_limit_bytes=32 * 1024 * 1024),
    )(*windows, est, edges, tops, rests)
    updated = est * jnp.exp(codes.astype(jnp.float32) * (1.0 / scale))
    return updated.reshape(estimate.shape)


def solution(mesh):
    placed = (
        P("tile", None, None),
        P("view", "tile", None, None),
        P("view", None),
        P("view"),
        P("view"),
    )
    return jax.shard_map(
        body, mesh=mesh, in_specs=placed, out_specs=P("tile", None, None), check_vma=False
    )
```

```python
import functools
import itertools
import math

import jax
import jax.numpy as jnp
from jax import lax
from jax.experimental import pallas as pl
from jax.experimental.pallas import tpu as pltpu
from jax.sharding import PartitionSpec as P

H = 6
TAIL, HEAD = H + 1, H
RADIX = 8
MESH = pl.DeviceIdType.MESH
HBM = pl.BlockSpec(memory_space=pltpu.HBM)
ANY = pl.BlockSpec(memory_space=pl.ANY)
SMEM = pl.BlockSpec(memory_space=pltpu.SMEM)
VMEM = pl.BlockSpec(memory_space=pltpu.VMEM)

profile_sigma = 48.0


def make_plan(views, tiles):
    size = 2 if tiles <= RADIX else 1
    plan = []
    for first in range(0, views, size):
        stride = 1
        while stride < tiles:
            digits = min(RADIX, -(-tiles // stride))
            plan.append((tuple(range(first, min(first + size, views))), stride, digits))
            stride *= digits
    return plan


def greet(partners):
    barrier = pltpu.get_barrier_semaphore()
    for partner in partners:
        pl.semaphore_signal(barrier, inc=1, device_id=partner, device_id_type=MESH)
    return lambda: pl.semaphore_wait(barrier, len(partners))


def exchange_kernel(views, tiles, plan, meas, est, profile, offset, shift, *refs):
    windows, (edges, tops, rests) = refs[:views], refs[views:views + 3]
    indices, infos = refs[views + 3:-11], refs[-11]
    slab, low, high, staged, frames, weights, info, send, recv, local = refs[-10:]
    v, t = lax.axis_index("view"), lax.axis_index("tile")
    rows = meas.shape[0]
    middle = rows - 2 * H
    sides = TAIL + HEAD
    reach = low.shape[0] - TAIL
    after, before = lax.rem(t + 1, tiles), lax.rem(t + tiles - 1, tiles)
    peers = [lax.rem(v + step, views) for step in range(views)]
    arrived = greet([(q, t) for q in peers[1:]] + [(v, after), (v, before)])
    loads = [pltpu.make_async_copy(meas, slab, local.at[0]),
             pltpu.make_async_copy(profile, weights, local.at[1])]
    for copy in loads:
        copy.start()

    def push(src, dst, kind, step, device):
        copy = pltpu.make_async_remote_copy(
            src_ref=src, dst_ref=dst, send_sem=send.at[kind, step], recv_sem=recv.at[kind, step],
            device_id=device, device_id_type=MESH)
        copy.start()
        return copy

    for copy in loads:
        copy.wait()
    row = lax.broadcasted_iota(jnp.int32, info.shape, 0)
    numbers = jnp.where(row == 1, offset[0].astype(jnp.float32) + 16.0, shift[0].astype(jnp.float32) + 1.0)
    info[...] = jnp.where(row == 0, jnp.broadcast_to(weights[...], info.shape), numbers)
    move = offset[0]
    arrived()
    halos = [
        push(slab.at[pl.ds(rows - TAIL, TAIL)], low.at[pl.ds(0, TAIL)], 2, 0, (v, after)),
        push(slab.at[pl.ds(0, HEAD)], high.at[pl.ds(reach, HEAD)], 2, 1, (v, before)),
    ]
    notes = [push(info, infos.at[v], 1, step, (peers[step], t)) for step in range(1, views)]
    copies = []
    for step in range(1, views):
        staged[step, pl.ds(0, middle)] = slab[pl.ds(H - move, middle), peers[step]]
        copies.append(push(staged.at[step, pl.ds(0, middle)], frames.at[v, pl.ds(0, middle)], 0, step, (peers[step], t)))
    copies.append(push(est.at[rows - 1, v], edges.at[0], 4, 0, (v, after)))
    copies.append(push(est.at[0, v], edges.at[1], 4, 1, (v, before)))
    frames[v, pl.ds(0, middle)] = slab[pl.ds(H - move, middle), v]
    infos[v] = info[...]
    low[pl.ds(TAIL, reach)] = slab[pl.ds(0, reach)]
    high[pl.ds(0, reach)] = slab[pl.ds(rows - reach, reach)]
    for copy in halos:
        copy.wait()
    for step in range(1, views):
        staged[step, pl.ds(middle, TAIL)] = low[pl.ds(H - move, TAIL), peers[step]]
        staged[step, pl.ds(middle + TAIL, HEAD)] = high[pl.ds(H - move, HEAD), peers[step]]
        copies.append(push(staged.at[step, pl.ds(middle, sides)], frames.at[v, pl.ds(middle, sides)], 3, step, (peers[step], t)))
    frames[v, pl.ds(middle, TAIL)] = low[pl.ds(H - move, TAIL), v]
    frames[v, pl.ds(middle + TAIL, HEAD)] = high[pl.ds(H - move, HEAD), v]
    for copy in notes:
        copy.wait()
    length = meas.shape[3]
    column = lax.broadcasted_iota(jnp.int32, info.shape, 1)
    distance = jnp.minimum(column, length - column).astype(jnp.float32)
    bell = jnp.exp(-distance * distance / (2.0 * profile_sigma * profile_sigma))
    for k in range(views):
        taps = infos[k] * bell
        taps = (taps / jnp.sum(taps, axis=1, keepdims=True))[0:1]
        table = pltpu.roll(jnp.broadcast_to(taps, (length, length)), 0, 1, stride=1, stride_axis=0)
        top, rest = split(table)
        tops[k] = top
        rests[k] = rest
    shifts = [infos[k, 2, 0].astype(jnp.int32) - 1 for k in range(views)]
    for (members, stride, digits), index in zip(plan, indices):
        total = 0
        for k in members:
            total = total * digits + shifts[k] // stride % digits
        index[0] = total
    for copy in copies:
        copy.wait()
    for k in range(views):
        windows[k][pl.ds(0, TAIL)] = frames[k, pl.ds(middle, TAIL)]
        windows[k][pl.ds(TAIL, middle)] = frames[k, pl.ds(0, middle)]
        windows[k][pl.ds(TAIL + middle, HEAD)] = frames[k, pl.ds(middle + TAIL, HEAD)]


def split(value):
    high = value.astype(jnp.bfloat16)
    return high, (value - high.astype(jnp.float32)).astype(jnp.bfloat16)


def blur(value, high, low, adjoint):
    dims = (((1,), (1 if adjoint else 0,)), ((), ()))
    dot = functools.partial(lax.dot_general, dimension_numbers=dims, preferred_element_type=jnp.float32)
    top, rest = split(value)
    return dot(top, high) + (dot(rest, high) + dot(top, low))


def update_kernel(views, chunk, scale, *refs):
    windows = refs[:views]
    own, edges, high, low, codes = refs[views:views + 5]
    est, coded, send, recv, local = refs[views + 5:]
    v, t = lax.axis_index("view"), lax.axis_index("tile")
    rows, _, share, length = own.shape
    peers = [lax.rem(v + step, views) for step in range(views)]
    arrived = greet([(q, t) for q in peers[1:]])
    est[pl.ds(0, 1)] = edges[pl.ds(0, 1)]
    est[pl.ds(1, rows)] = own[:, v]
    est[pl.ds(rows + 1, 1)] = edges[pl.ds(1, 1)]
    arrived()

    relay = views == 4 and chunk % 2 == 0
    near = [v + 1 - 2 * lax.rem(v, 2), lax.rem(v + 2, 4)] if relay else peers[1:]

    def copy_of(i, step):
        part = pl.ds(i * chunk, chunk)
        return pltpu.make_async_remote_copy(
            src_ref=coded.at[part], dst_ref=codes.at[part, v],
            send_sem=send.at[i, step], recv_sem=recv.at[i, step],
            device_id=(near[step], t), device_id_type=MESH)

    def passed(i, step):
        part = pl.ds(i * chunk + step * (chunk // 2), chunk // 2)
        block = codes.at[part, near[step]]
        return pltpu.make_async_remote_copy(
            src_ref=block, dst_ref=block,
            send_sem=send.at[i, 2 + step], recv_sem=recv.at[i, 2 + step],
            device_id=(near[1 - step], t), device_id_type=MESH)

    def pass_on(i):
        for step in range(2):
            copy_of(i, step).wait_recv()
            passed(i, step).start()

    def kept(i):
        part = pl.ds(i * chunk, chunk)
        return pltpu.make_async_copy(coded.at[part], codes.at[part, v], local.at[i])

    def work(i, carry):
        at = i * chunk
        product = None
        for k in range(views):
            mix = (k + 1) / (views + 1)
            warped = mix * est[pl.ds(at, chunk + 1)] + (1 - mix) * est[pl.ds(at + 1, chunk + 1)]
            flat = warped.reshape((chunk + 1) * share, length)
            forward = blur(flat, high[k], low[k], False)
            seen = windows[k][pl.ds(at, chunk + 1)].astype(jnp.float32)
            ratios = seen.reshape(flat.shape) / forward
            back = blur(ratios, high[k], low[k], True).reshape(chunk + 1, share, length)
            term = mix * back[1:] + (1 - mix) * back[:-1]
            product = term if product is None else product * term
        code = jnp.round(jnp.log(product) * scale)
        coded[pl.ds(at, chunk)] = code.astype(jnp.int32).astype(jnp.int16)
        for step in range(len(near)):
            copy_of(i, step).start()
        kept(i).start()
        if relay:
            @pl.when(i > 0)
            def _():
                pass_on(i - 1)
        return carry

    lax.fori_loop(0, rows // chunk, work, 0)
    if relay:
        pass_on(rows // chunk - 1)

    def finish(i, carry):
        for step in range(len(near)):
            if relay:
                copy_of(i, step).wait_send()
                passed(i, step).wait()
            else:
                copy_of(i, step).wait()
        kept(i).wait()
        return carry

    lax.fori_loop(0, rows // chunk, finish, 0)


def body(estimate, measured, blur_profile, view_offset, tile_shift):
    views, tiles = lax.axis_size("view"), lax.axis_size("tile")
    rows, height, length = estimate.shape
    share = height // views
    scale = 32767.0 / (views * 1.4)
    shape = jax.ShapeDtypeStruct
    plan = make_plan(views, tiles)

    meas = measured[0].reshape(rows, views, share, length)
    est = estimate.reshape(rows, views, share, length)
    out = pl.pallas_call(
        functools.partial(exchange_kernel, views, tiles, plan),
        out_shape=[shape((rows + 1, share, length), jnp.bfloat16)] * views + [
            shape((2, share, length), jnp.float32),
            shape((views, length, length), jnp.bfloat16),
            shape((views, length, length), jnp.bfloat16),
        ] + [shape((1,), jnp.int32)] * len(plan),
        in_specs=[HBM, HBM, HBM, SMEM, SMEM],
        out_specs=[VMEM] * (views + 3) + [SMEM] * len(plan),
        scratch_shapes=[
            pltpu.VMEM((views, 8, length), jnp.float32),
            pltpu.VMEM((rows, views, share, length), jnp.bfloat16),
            pltpu.VMEM((TAIL + 2 * H, views, share, length), jnp.bfloat16),
            pltpu.VMEM((HEAD + 2 * H, views, share, length), jnp.bfloat16),
            pltpu.VMEM((views, rows + 1, share, length), jnp.bfloat16),
            pltpu.VMEM((views, rows + 1, share, length), jnp.bfloat16),
            pltpu.VMEM((1, length), jnp.float32),
            pltpu.VMEM((8, length), jnp.float32),
            pltpu.SemaphoreType.DMA((5, max(views, 2))),
            pltpu.SemaphoreType.DMA((5, max(views, 2))),
            pltpu.SemaphoreType.DMA((2,)),
        ],
        compiler_params=pltpu.CompilerParams(
            collective_id=0, has_side_effects=True, vmem_limit_bytes=54 * 1024 * 1024),
    )(meas, est, blur_profile, view_offset, tile_shift)
    windows, (edges, tops, rests, *indices) = out[:views], out[views:]

    def moved(distance, window):
        if distance == 0:
            return window
        return lax.ppermute(window, "tile", [(i, (i + distance) % tiles) for i in range(tiles)])

    def route(distances, *group):
        return tuple(moved(d, window) for d, window in zip(distances, group))

    windows = list(windows)
    for (members, stride, digits), index in zip(plan, indices):
        routes = [functools.partial(route, [stride * d for d in distances])
                  for distances in itertools.product(range(digits), repeat=len(members))]
        group = lax.switch(index[0], routes, *[windows[k] for k in members])
        for k, window in zip(members, group):
            windows[k] = window

    chunk = 8
    pieces = rows // chunk
    codes = pl.pallas_call(
        functools.partial(update_kernel, views, chunk, scale),
        out_shape=shape((rows, views, share, length), jnp.int16),
        in_specs=[VMEM] * (views + 4),
        out_specs=ANY,
        scratch_shapes=[
            pltpu.VMEM((rows + 2, share, length), jnp.float32),
            pltpu.VMEM((rows, share, length), jnp.int16),
            pltpu.SemaphoreType.DMA((pieces, views)),
            pltpu.SemaphoreType.DMA((pieces, views)),
            pltpu.SemaphoreType.DMA((pieces,)),
        ],
        compiler_params=pltpu.CompilerParams(
            collective_id=1, has_side_effects=True, vmem_limit_bytes=32 * 1024 * 1024),
    )(*windows, est, edges, tops, rests)
    updated = est * jnp.exp(codes.astype(jnp.float32) * (1.0 / scale))
    return updated.reshape(estimate.shape)


def solution(mesh):
    placed = (
        P("tile", None, None),
        P("view", "tile", None, None),
        P("view", None),
        P("view"),
        P("view"),
    )
    return jax.shard_map(
        body, mesh=mesh, in_specs=placed, out_specs=P("tile", None, None), check_vma=False
    )
```

```python
import functools
import itertools
import math

import jax
import jax.numpy as jnp
from jax import lax
from jax.experimental import pallas as pl
from jax.experimental.pallas import tpu as pltpu
from jax.sharding import PartitionSpec as P

H = 6
TAIL, HEAD = H + 1, H
RADIX = 8
MESH = pl.DeviceIdType.MESH
HBM = pl.BlockSpec(memory_space=pltpu.HBM)
ANY = pl.BlockSpec(memory_space=pl.ANY)
SMEM = pl.BlockSpec(memory_space=pltpu.SMEM)
VMEM = pl.BlockSpec(memory_space=pltpu.VMEM)

profile_sigma = 48.0


def make_plan(views, tiles):
    size = 2 if tiles <= RADIX else 1
    plan = []
    for first in range(0, views, size):
        stride = 1
        while stride < tiles:
            digits = min(RADIX, -(-tiles // stride))
            plan.append((tuple(range(first, min(first + size, views))), stride, digits))
            stride *= digits
    return plan


def greet(partners):
    barrier = pltpu.get_barrier_semaphore()
    for partner in partners:
        pl.semaphore_signal(barrier, inc=1, device_id=partner, device_id_type=MESH)
    return lambda: pl.semaphore_wait(barrier, len(partners))


def exchange_kernel(views, tiles, plan, meas, est, profile, offset, shift, *refs):
    windows, (edges, tops, rests) = refs[:views], refs[views:views + 3]
    indices, infos = refs[views + 3:-11], refs[-11]
    slab, low, high, staged, frames, weights, info, send, recv, local = refs[-10:]
    v, t = lax.axis_index("view"), lax.axis_index("tile")
    rows = meas.shape[0]
    middle = rows - 2 * H
    sides = TAIL + HEAD
    reach = low.shape[0] - TAIL
    after, before = lax.rem(t + 1, tiles), lax.rem(t + tiles - 1, tiles)
    peers = [lax.rem(v + step, views) for step in range(views)]
    arrived = greet([(q, t) for q in peers[1:]] + [(v, after), (v, before)])
    loads = [pltpu.make_async_copy(meas, slab, local.at[0]),
             pltpu.make_async_copy(profile, weights, local.at[1])]
    for copy in loads:
        copy.start()

    def push(src, dst, kind, step, device):
        copy = pltpu.make_async_remote_copy(
            src_ref=src, dst_ref=dst, send_sem=send.at[kind, step], recv_sem=recv.at[kind, step],
            device_id=device, device_id_type=MESH)
        copy.start()
        return copy

    for copy in loads:
        copy.wait()
    row = lax.broadcasted_iota(jnp.int32, info.shape, 0)
    numbers = jnp.where(row == 1, offset[0].astype(jnp.float32) + 16.0, shift[0].astype(jnp.float32) + 1.0)
    info[...] = jnp.where(row == 0, jnp.broadcast_to(weights[...], info.shape), numbers)
    move = offset[0]
    arrived()
    halos = [
        push(slab.at[pl.ds(rows - TAIL, TAIL)], low.at[pl.ds(0, TAIL)], 2, 0, (v, after)),
        push(slab.at[pl.ds(0, HEAD)], high.at[pl.ds(reach, HEAD)], 2, 1, (v, before)),
    ]
    notes = [push(info, infos.at[v], 1, step, (peers[step], t)) for step in range(1, views)]
    copies = []
    for step in range(1, views):
        staged[step, pl.ds(0, middle)] = slab[pl.ds(H - move, middle), peers[step]]
        copies.append(push(staged.at[step, pl.ds(0, middle)], frames.at[v, pl.ds(0, middle)], 0, step, (peers[step], t)))
    copies.append(push(est.at[rows - 1, v], edges.at[0], 4, 0, (v, after)))
    copies.append(push(est.at[0, v], edges.at[1], 4, 1, (v, before)))
    frames[v, pl.ds(0, middle)] = slab[pl.ds(H - move, middle), v]
    infos[v] = info[...]
    low[pl.ds(TAIL, reach)] = slab[pl.ds(0, reach)]
    high[pl.ds(0, reach)] = slab[pl.ds(rows - reach, reach)]
    for copy in halos:
        copy.wait()
    for step in range(1, views):
        staged[step, pl.ds(middle, TAIL)] = low[pl.ds(H - move, TAIL), peers[step]]
        staged[step, pl.ds(middle + TAIL, HEAD)] = high[pl.ds(H - move, HEAD), peers[step]]
        copies.append(push(staged.at[step, pl.ds(middle, sides)], frames.at[v, pl.ds(middle, sides)], 3, step, (peers[step], t)))
    frames[v, pl.ds(middle, TAIL)] = low[pl.ds(H - move, TAIL), v]
    frames[v, pl.ds(middle + TAIL, HEAD)] = high[pl.ds(H - move, HEAD), v]
    for copy in notes:
        copy.wait()
    length = meas.shape[3]
    column = lax.broadcasted_iota(jnp.int32, info.shape, 1)
    distance = jnp.minimum(column, length - column).astype(jnp.float32)
    bell = jnp.exp(-distance * distance / (2.0 * profile_sigma * profile_sigma))
    for k in range(views):
        taps = infos[k] * bell
        taps = (taps / jnp.sum(taps, axis=1, keepdims=True))[0:1]
        table = pltpu.roll(jnp.broadcast_to(taps, (length, length)), 0, 1, stride=1, stride_axis=0)
        for at, part in ((k, table), (views + k, table.T)):
            top, rest = split(part)
            tops[at] = top
            rests[at] = rest
    shifts = [infos[k, 2, 0].astype(jnp.int32) - 1 for k in range(views)]
    for (members, stride, digits), index in zip(plan, indices):
        total = 0
        for k in members:
            total = total * digits + shifts[k] // stride % digits
        index[0] = total
    for copy in copies:
        copy.wait()
    for k in range(views):
        windows[k][pl.ds(0, TAIL)] = frames[k, pl.ds(middle, TAIL)]
        windows[k][pl.ds(TAIL, middle)] = frames[k, pl.ds(0, middle)]
        windows[k][pl.ds(TAIL + middle, HEAD)] = frames[k, pl.ds(middle + TAIL, HEAD)]


def split(value):
    high = value.astype(jnp.bfloat16)
    return high, (value - high.astype(jnp.float32)).astype(jnp.bfloat16)


def blur(value, high, low):
    top, rest = split(value)
    count = value.shape[0]
    dot = functools.partial(jnp.dot, preferred_element_type=jnp.float32)
    both = dot(jnp.concatenate([top, rest], axis=0), high)
    return both[:count] + (both[count:] + dot(top, low))


def update_kernel(views, chunk, scale, *refs):
    windows = refs[:views]
    own, edges, high, low, codes = refs[views:views + 5]
    est, coded, send, recv, local = refs[views + 5:]
    v, t = lax.axis_index("view"), lax.axis_index("tile")
    rows, _, share, length = own.shape
    peers = [lax.rem(v + step, views) for step in range(views)]
    arrived = greet([(q, t) for q in peers[1:]])
    est[pl.ds(0, 1)] = edges[pl.ds(0, 1)]
    est[pl.ds(1, rows)] = own[:, v]
    est[pl.ds(rows + 1, 1)] = edges[pl.ds(1, 1)]
    arrived()

    relay = views == 4 and chunk % 2 == 0
    near = [v + 1 - 2 * lax.rem(v, 2), lax.rem(v + 2, 4)] if relay else peers[1:]

    def copy_of(i, step):
        part = pl.ds(i * chunk, chunk)
        return pltpu.make_async_remote_copy(
            src_ref=coded.at[part], dst_ref=codes.at[part, v],
            send_sem=send.at[i, step], recv_sem=recv.at[i, step],
            device_id=(near[step], t), device_id_type=MESH)

    def passed(i, step):
        part = pl.ds(i * chunk + step * (chunk // 2), chunk // 2)
        block = codes.at[part, near[step]]
        return pltpu.make_async_remote_copy(
            src_ref=block, dst_ref=block,
            send_sem=send.at[i, 2 + step], recv_sem=recv.at[i, 2 + step],
            device_id=(near[1 - step], t), device_id_type=MESH)

    def pass_on(i):
        for step in range(2):
            copy_of(i, step).wait_recv()
            passed(i, step).start()

    def kept(i):
        part = pl.ds(i * chunk, chunk)
        return pltpu.make_async_copy(coded.at[part], codes.at[part, v], local.at[i])

    def work(i, carry):
        at = i * chunk
        product = None
        for k in range(views):
            mix = (k + 1) / (views + 1)
            warped = mix * est[pl.ds(at, chunk + 1)] + (1 - mix) * est[pl.ds(at + 1, chunk + 1)]
            flat = warped.reshape((chunk + 1) * share, length)
            forward = blur(flat, high[k], low[k])
            seen = windows[k][pl.ds(at, chunk + 1)].astype(jnp.float32)
            ratios = seen.reshape(flat.shape) / forward
            back = blur(ratios, high[views + k], low[views + k]).reshape(chunk + 1, share, length)
            term = mix * back[1:] + (1 - mix) * back[:-1]
            product = term if product is None else product * term
        code = jnp.round(jnp.log(product) * scale)
        coded[pl.ds(at, chunk)] = code.astype(jnp.int32).astype(jnp.int16)
        for step in range(len(near)):
            copy_of(i, step).start()
        kept(i).start()
        if relay:
            @pl.when(i > 0)
            def _():
                pass_on(i - 1)
        return carry

    lax.fori_loop(0, rows // chunk, work, 0)
    if relay:
        pass_on(rows // chunk - 1)

    def finish(i, carry):
        for step in range(len(near)):
            if relay:
                copy_of(i, step).wait_send()
                passed(i, step).wait()
            else:
                copy_of(i, step).wait()
        kept(i).wait()
        return carry

    lax.fori_loop(0, rows // chunk, finish, 0)


def body(estimate, measured, blur_profile, view_offset, tile_shift):
    views, tiles = lax.axis_size("view"), lax.axis_size("tile")
    rows, height, length = estimate.shape
    share = height // views
    scale = 32767.0 / (views * 1.4)
    shape = jax.ShapeDtypeStruct
    plan = make_plan(views, tiles)

    meas = measured[0].reshape(rows, views, share, length)
    est = estimate.reshape(rows, views, share, length)
    out = pl.pallas_call(
        functools.partial(exchange_kernel, views, tiles, plan),
        out_shape=[shape((rows + 1, share, length), jnp.bfloat16)] * views + [
            shape((2, share, length), jnp.float32),
            shape((2 * views, length, length), jnp.bfloat16),
            shape((2 * views, length, length), jnp.bfloat16),
        ] + [shape((1,), jnp.int32)] * len(plan),
        in_specs=[HBM, HBM, HBM, SMEM, SMEM],
        out_specs=[VMEM] * (views + 3) + [SMEM] * len(plan),
        scratch_shapes=[
            pltpu.VMEM((views, 8, length), jnp.float32),
            pltpu.VMEM((rows, views, share, length), jnp.bfloat16),
            pltpu.VMEM((TAIL + 2 * H, views, share, length), jnp.bfloat16),
            pltpu.VMEM((HEAD + 2 * H, views, share, length), jnp.bfloat16),
            pltpu.VMEM((views, rows + 1, share, length), jnp.bfloat16),
            pltpu.VMEM((views, rows + 1, share, length), jnp.bfloat16),
            pltpu.VMEM((1, length), jnp.float32),
            pltpu.VMEM((8, length), jnp.float32),
            pltpu.SemaphoreType.DMA((5, max(views, 2))),
            pltpu.SemaphoreType.DMA((5, max(views, 2))),
            pltpu.SemaphoreType.DMA((2,)),
        ],
        compiler_params=pltpu.CompilerParams(
            collective_id=0, has_side_effects=True, vmem_limit_bytes=40 * 1024 * 1024),
    )(meas, est, blur_profile, view_offset, tile_shift)
    windows, (edges, tops, rests, *indices) = out[:views], out[views:]

    def moved(distance, window):
        if distance == 0:
            return window
        return lax.ppermute(window, "tile", [(i, (i + distance) % tiles) for i in range(tiles)])

    def route(distances, *group):
        return tuple(moved(d, window) for d, window in zip(distances, group))

    windows = list(windows)
    for (members, stride, digits), index in zip(plan, indices):
        routes = [functools.partial(route, [stride * d for d in distances])
                  for distances in itertools.product(range(digits), repeat=len(members))]
        group = lax.switch(index[0], routes, *[windows[k] for k in members])
        for k, window in zip(members, group):
            windows[k] = window

    chunk = 8
    pieces = rows // chunk
    codes = pl.pallas_call(
        functools.partial(update_kernel, views, chunk, scale),
        out_shape=shape((rows, views, share, length), jnp.int16),
        in_specs=[VMEM] * (views + 4),
        out_specs=ANY,
        scratch_shapes=[
            pltpu.VMEM((rows + 2, share, length), jnp.float32),
            pltpu.VMEM((rows, share, length), jnp.int16),
            pltpu.SemaphoreType.DMA((pieces, views)),
            pltpu.SemaphoreType.DMA((pieces, views)),
            pltpu.SemaphoreType.DMA((pieces,)),
        ],
        compiler_params=pltpu.CompilerParams(
            collective_id=1, has_side_effects=True, vmem_limit_bytes=32 * 1024 * 1024),
    )(*windows, est, edges, tops, rests)
    updated = est * jnp.exp(codes.astype(jnp.float32) * (1.0 / scale))
    return updated.reshape(estimate.shape)


def solution(mesh):
    placed = (
        P("tile", None, None),
        P("view", "tile", None, None),
        P("view", None),
        P("view"),
        P("view"),
    )
    return jax.shard_map(
        body, mesh=mesh, in_specs=placed, out_specs=P("tile", None, None), check_vma=False
    )
```

```python
import functools
import itertools
import math

import jax
import jax.numpy as jnp
from jax import lax
from jax.experimental import pallas as pl
from jax.experimental.pallas import tpu as pltpu
from jax.sharding import PartitionSpec as P

H = 6
TAIL, HEAD = H + 1, H
RADIX = 8
MESH = pl.DeviceIdType.MESH
HBM = pl.BlockSpec(memory_space=pltpu.HBM)
ANY = pl.BlockSpec(memory_space=pl.ANY)
SMEM = pl.BlockSpec(memory_space=pltpu.SMEM)
VMEM = pl.BlockSpec(memory_space=pltpu.VMEM)

profile_sigma = 48.0


def make_plan(views, tiles):
    size = 2 if tiles <= RADIX else 1
    plan = []
    for first in range(0, views, size):
        stride = 1
        while stride < tiles:
            digits = min(RADIX, -(-tiles // stride))
            plan.append((tuple(range(first, min(first + size, views))), stride, digits))
            stride *= digits
    return plan


def greet(partners):
    barrier = pltpu.get_barrier_semaphore()
    for partner in partners:
        pl.semaphore_signal(barrier, inc=1, device_id=partner, device_id_type=MESH)
    return lambda: pl.semaphore_wait(barrier, len(partners))


def exchange_kernel(views, tiles, plan, meas, est, profile, offset, shift, *refs):
    windows, (edges, tops, rests) = refs[:views], refs[views:views + 3]
    indices, infos = refs[views + 3:-11], refs[-11]
    slab, low, high, staged, frames, weights, info, send, recv, local = refs[-10:]
    v, t = lax.axis_index("view"), lax.axis_index("tile")
    rows = meas.shape[0]
    middle = rows - 2 * H
    sides = TAIL + HEAD
    reach = low.shape[0] - TAIL
    after, before = lax.rem(t + 1, tiles), lax.rem(t + tiles - 1, tiles)
    peers = [lax.rem(v + step, views) for step in range(views)]
    arrived = greet([(q, t) for q in peers[1:]] + [(v, after), (v, before)])
    loads = [pltpu.make_async_copy(meas, slab, local.at[0]),
             pltpu.make_async_copy(profile, weights, local.at[1])]
    for copy in loads:
        copy.start()

    def push(src, dst, kind, step, device):
        copy = pltpu.make_async_remote_copy(
            src_ref=src, dst_ref=dst, send_sem=send.at[kind, step], recv_sem=recv.at[kind, step],
            device_id=device, device_id_type=MESH)
        copy.start()
        return copy

    for copy in loads:
        copy.wait()
    row = lax.broadcasted_iota(jnp.int32, info.shape, 0)
    numbers = jnp.where(row == 1, offset[0].astype(jnp.float32) + 16.0, shift[0].astype(jnp.float32) + 1.0)
    info[...] = jnp.where(row == 0, jnp.broadcast_to(weights[...], info.shape), numbers)
    move = offset[0]
    arrived()
    halos = [
        push(slab.at[pl.ds(rows - TAIL, TAIL)], low.at[pl.ds(0, TAIL)], 2, 0, (v, after)),
        push(slab.at[pl.ds(0, HEAD)], high.at[pl.ds(reach, HEAD)], 2, 1, (v, before)),
    ]
    notes = [push(info, infos.at[v], 1, step, (peers[step], t)) for step in range(1, views)]
    copies = []
    for step in range(1, views):
        staged[step, pl.ds(0, middle)] = slab[pl.ds(H - move, middle), peers[step]]
        copies.append(push(staged.at[step, pl.ds(0, middle)], frames.at[v, pl.ds(0, middle)], 0, step, (peers[step], t)))
    copies.append(push(est.at[rows - 1, v], edges.at[0], 4, 0, (v, after)))
    copies.append(push(est.at[0, v], edges.at[1], 4, 1, (v, before)))
    frames[v, pl.ds(0, middle)] = slab[pl.ds(H - move, middle), v]
    infos[v] = info[...]
    low[pl.ds(TAIL, reach)] = slab[pl.ds(0, reach)]
    high[pl.ds(0, reach)] = slab[pl.ds(rows - reach, reach)]
    for copy in halos:
        copy.wait()
    for step in range(1, views):
        staged[step, pl.ds(middle, TAIL)] = low[pl.ds(H - move, TAIL), peers[step]]
        staged[step, pl.ds(middle + TAIL, HEAD)] = high[pl.ds(H - move, HEAD), peers[step]]
        copies.append(push(staged.at[step, pl.ds(middle, sides)], frames.at[v, pl.ds(middle, sides)], 3, step, (peers[step], t)))
    frames[v, pl.ds(middle, TAIL)] = low[pl.ds(H - move, TAIL), v]
    frames[v, pl.ds(middle + TAIL, HEAD)] = high[pl.ds(H - move, HEAD), v]
    for copy in notes:
        copy.wait()
    length = meas.shape[3]
    column = lax.broadcasted_iota(jnp.int32, info.shape, 1)
    distance = jnp.minimum(column, length - column).astype(jnp.float32)
    bell = jnp.exp(-distance * distance / (2.0 * profile_sigma * profile_sigma))
    for k in range(views):
        taps = infos[k] * bell
        taps = (taps / jnp.sum(taps, axis=1, keepdims=True))[0:1]
        table = pltpu.roll(jnp.broadcast_to(taps, (length, length)), 0, 1, stride=1, stride_axis=0)
        for at, part in ((k, table), (views + k, table.T)):
            top, rest = split(part)
            tops[at] = top
            rests[at] = rest
    shifts = [infos[k, 2, 0].astype(jnp.int32) - 1 for k in range(views)]
    for (members, stride, digits), index in zip(plan, indices):
        total = 0
        for k in members:
            total = total * digits + shifts[k] // stride % digits
        index[0] = total
    for copy in copies:
        copy.wait()
    for k in range(views):
        windows[k][pl.ds(0, TAIL)] = frames[k, pl.ds(middle, TAIL)]
        windows[k][pl.ds(TAIL, middle)] = frames[k, pl.ds(0, middle)]
        windows[k][pl.ds(TAIL + middle, HEAD)] = frames[k, pl.ds(middle + TAIL, HEAD)]


def split(value):
    high = value.astype(jnp.bfloat16)
    return high, (value - high.astype(jnp.float32)).astype(jnp.bfloat16)


def blur(value, high, low):
    top, rest = split(value)
    count = value.shape[0]
    dot = functools.partial(jnp.dot, preferred_element_type=jnp.float32)
    both = dot(jnp.concatenate([top, rest], axis=0), high)
    return both[:count] + (both[count:] + dot(top, low))


def update_kernel(views, chunk, scale, *refs):
    windows = refs[:views]
    own, edges, high, low, codes = refs[views:views + 5]
    est, coded, send, recv, local = refs[views + 5:]
    v, t = lax.axis_index("view"), lax.axis_index("tile")
    rows, _, share, length = own.shape
    peers = [lax.rem(v + step, views) for step in range(views)]
    arrived = greet([(q, t) for q in peers[1:]])
    est[pl.ds(0, 1)] = edges[pl.ds(0, 1)]
    est[pl.ds(1, rows)] = own[:, v]
    est[pl.ds(rows + 1, 1)] = edges[pl.ds(1, 1)]
    arrived()

    relay = views == 4 and chunk % 2 == 0
    near = [v + 1 - 2 * lax.rem(v, 2), lax.rem(v + 2, 4)] if relay else peers[1:]

    def copy_of(i, step):
        part = pl.ds(i * chunk, chunk)
        return pltpu.make_async_remote_copy(
            src_ref=coded.at[part], dst_ref=codes.at[part, v],
            send_sem=send.at[i, step], recv_sem=recv.at[i, step],
            device_id=(near[step], t), device_id_type=MESH)

    def passed(i, step):
        part = pl.ds(i * chunk + step * (chunk // 2), chunk // 2)
        block = codes.at[part, near[step]]
        return pltpu.make_async_remote_copy(
            src_ref=block, dst_ref=block,
            send_sem=send.at[i, 2 + step], recv_sem=recv.at[i, 2 + step],
            device_id=(near[1 - step], t), device_id_type=MESH)

    def pass_on(i):
        for step in range(2):
            copy_of(i, step).wait_recv()
            passed(i, step).start()

    def kept(i):
        part = pl.ds(i * chunk, chunk)
        return pltpu.make_async_copy(coded.at[part], codes.at[part, v], local.at[i])

    def work(i, carry):
        at = i * chunk
        product = None
        for k in range(views):
            mix = (k + 1) / (views + 1)
            warped = mix * est[pl.ds(at, chunk + 1)] + (1 - mix) * est[pl.ds(at + 1, chunk + 1)]
            flat = warped.reshape((chunk + 1) * share, length)
            forward = blur(flat, high[k], low[k])
            seen = windows[k][pl.ds(at, chunk + 1)].astype(jnp.float32)
            ratios = seen.reshape(flat.shape) / forward
            back = blur(ratios, high[views + k], low[views + k]).reshape(chunk + 1, share, length)
            term = mix * back[1:] + (1 - mix) * back[:-1]
            product = term if product is None else product * term
        code = jnp.round(jnp.log(product) * scale)
        coded[pl.ds(at, chunk)] = code.astype(jnp.int32).astype(jnp.int16)
        for step in range(len(near)):
            copy_of(i, step).start()
        kept(i).start()
        if relay:
            @pl.when(i > 0)
            def _():
                pass_on(i - 1)
        return carry

    lax.fori_loop(0, rows // chunk, work, 0)
    if relay:
        pass_on(rows // chunk - 1)

    def finish(i, carry):
        for step in range(len(near)):
            if relay:
                copy_of(i, step).wait_send()
                passed(i, step).wait()
            else:
                copy_of(i, step).wait()
        kept(i).wait()
        return carry

    lax.fori_loop(0, rows // chunk, finish, 0)


def body(estimate, measured, blur_profile, view_offset, tile_shift):
    views, tiles = lax.axis_size("view"), lax.axis_size("tile")
    rows, height, length = estimate.shape
    share = height // views
    scale = 32767.0 / (views * 1.4)
    shape = jax.ShapeDtypeStruct
    plan = make_plan(views, tiles)

    meas = measured[0].reshape(rows, views, share, length)
    est = estimate.reshape(rows, views, share, length)
    out = pl.pallas_call(
        functools.partial(exchange_kernel, views, tiles, plan),
        out_shape=[shape((rows + 1, share, length), jnp.bfloat16)] * views + [
            shape((2, share, length), jnp.float32),
            shape((2 * views, length, length), jnp.bfloat16),
            shape((2 * views, length, length), jnp.bfloat16),
        ] + [shape((1,), jnp.int32)] * len(plan),
        in_specs=[HBM, HBM, HBM, SMEM, SMEM],
        out_specs=[VMEM] * (views + 3) + [SMEM] * len(plan),
        scratch_shapes=[
            pltpu.VMEM((views, 8, length), jnp.float32),
            pltpu.VMEM((rows, views, share, length), jnp.bfloat16),
            pltpu.VMEM((TAIL + 2 * H, views, share, length), jnp.bfloat16),
            pltpu.VMEM((HEAD + 2 * H, views, share, length), jnp.bfloat16),
            pltpu.VMEM((views, rows + 1, share, length), jnp.bfloat16),
            pltpu.VMEM((views, rows + 1, share, length), jnp.bfloat16),
            pltpu.VMEM((1, length), jnp.float32),
            pltpu.VMEM((8, length), jnp.float32),
            pltpu.SemaphoreType.DMA((5, max(views, 2))),
            pltpu.SemaphoreType.DMA((5, max(views, 2))),
            pltpu.SemaphoreType.DMA((2,)),
        ],
        compiler_params=pltpu.CompilerParams(
            collective_id=0, has_side_effects=True, vmem_limit_bytes=60 * 1024 * 1024),
    )(meas, est, blur_profile, view_offset, tile_shift)
    windows, (edges, tops, rests, *indices) = out[:views], out[views:]

    def moved(distance, window):
        if distance == 0:
            return window
        return lax.ppermute(window, "tile", [(i, (i + distance) % tiles) for i in range(tiles)])

    def route(distances, *group):
        return tuple(moved(d, window) for d, window in zip(distances, group))

    windows = list(windows)
    for (members, stride, digits), index in zip(plan, indices):
        routes = [functools.partial(route, [stride * d for d in distances])
                  for distances in itertools.product(range(digits), repeat=len(members))]
        group = lax.switch(index[0], routes, *[windows[k] for k in members])
        for k, window in zip(members, group):
            windows[k] = window

    chunk = 8
    pieces = rows // chunk
    codes = pl.pallas_call(
        functools.partial(update_kernel, views, chunk, scale),
        out_shape=shape((rows, views, share, length), jnp.int16),
        in_specs=[VMEM] * (views + 4),
        out_specs=ANY,
        scratch_shapes=[
            pltpu.VMEM((rows + 2, share, length), jnp.float32),
            pltpu.VMEM((rows, share, length), jnp.int16),
            pltpu.SemaphoreType.DMA((pieces, views)),
            pltpu.SemaphoreType.DMA((pieces, views)),
            pltpu.SemaphoreType.DMA((pieces,)),
        ],
        compiler_params=pltpu.CompilerParams(
            collective_id=1, has_side_effects=True, vmem_limit_bytes=32 * 1024 * 1024),
    )(*windows, est, edges, tops, rests)
    updated = est * jnp.exp(codes.astype(jnp.float32) * (1.0 / scale))
    return updated.reshape(estimate.shape)


def solution(mesh):
    placed = (
        P("tile", None, None),
        P("view", "tile", None, None),
        P("view", None),
        P("view"),
        P("view"),
    )
    return jax.shard_map(
        body, mesh=mesh, in_specs=placed, out_specs=P("tile", None, None), check_vma=False
    )
```
